256 devices in a mesh: grp: 32 (over z, x), box: 8 (over y, core).
Axes of the slice: x: 4, y: 4, z: 8, core: 2. Of those that a mesh axis runs over, the one named last changes fastest.
Arguments:
- source_term: float32 [53, 32, 16, 256], P(None, 'grp', 'box'), may hold values from -24 to 24
- diffusion: float32 [53], replicated, may hold values from 0.1 to 2
- stoich: float32 [53, 325], replicated, may hold values from -0.3125 to 0.3125
- orders: float32 [325, 53], replicated, may hold values from -0.875 to 0.875
- rates: float32 [325, 32, 16, 256], P(None, 'grp', 'box'), may hold values from 0.1 to 1
- precond: bfloat16 [53, 53, 32, 16, 256], P(None, None, 'grp', 'box'), may hold values from -1 to 1
- coarse_field: float32 [53, 32, 2048], P(None, 'grp', 'box'), may hold values from -6 to 6
- neighbours: int32 [32, 4], replicated, may hold values from -1 to 31, as said below
- ghost_list: int32 [32, 8, 160], P(None, 'box'), may hold values from -1 to 8191, as said below
- average_list: int32 [32, 8], P(None, 'box'), may hold values from 0 to 127, as said below
Outputs:
- correction: float32 [53, 32, 16, 256], P(None, 'grp', 'box')
- coarse_update: float32 [53, 32, 2048], P(None, 'grp', 'box')
The draws below stay inside these ranges and needn't reach their ends.
Inputs may be any that keep to these rules, and one draw needn't show every extreme that they name: Column g sits at one position of a grid 4 columns wide and 8 rows tall, each position taken once; neighbours[g, 0] and neighbours[g, 1] are the columns before and after it in its grid row, neighbours[g, 2] and neighbours[g, 3] the ones in the grid rows below and above, -1 at the grid's edge. The relation is symmetric: neighbours[neighbours[g, f], f xor 1] = g. `ghost_list`: an entry is -1 exactly where its face meets another fine sub-box: the lower x face for b > 0, the upper x face for b < 7, side face f where neighbours[g, f] >= 0. Every other entry is o * 256 + c, coarse cell c of the patch of column o at the same box index. `average_list`: entry o * 4 + j names block j of the patch of column o at the same box index; at each box index the 32 entries are distinct.
All inputs are finite; a program needn't handle non-finite values.
Results may differ from the reference program's by a relative error of at most 0.0007.
Values sent between devices are 32-bit elements; how exact they have to be, the bound alone decides.
No kernel may reach another device: no remote copies, remote signals or barrier semaphores. Data moves between devices by JAX's collectives and lax.ppermute only.
A program may use at most 64 MiB of HBM per device.

```python
import math
import jax
import jax.numpy as jnp
from jax import lax

S = 53
R = 325
FS = 16
CX = 2
ITERS = 4
CBLK = 4
GROUPS = 32
BOXES = 8
FACE = 256
XFACE_C = 64
SIDE_C = 8
GHOSTS = 160
BLOCK_C = 64
COARSE = 256


def column_layout(key):
    order = jax.random.permutation(key, GROUPS).astype(jnp.int32)
    spot = jnp.argsort(order, stable=True).astype(jnp.int32)
    column = spot % 4
    line = spot // 4
    targets = jnp.stack([spot - 1, spot + 1, spot - 4, spot + 4], axis=1)
    inside = jnp.stack([column > 0, column < 3, line > 0, line < GROUPS // 4 - 1], axis=1)
    found = order[jnp.clip(targets, 0, GROUPS - 1)]
    return jnp.where(inside, found, -1).astype(jnp.int32)


def draw_neighbours(key, part):
    return column_layout(key)


def draw_ghost_list(key, part):
    links = column_layout(key)
    key = jax.random.fold_in(key, 11)
    first_key, second_key = jax.random.split(key)
    owner = jax.random.randint(first_key, (GROUPS, BOXES, GHOSTS), 0, GROUPS)
    cell = jax.random.randint(second_key, (GROUPS, BOXES, GHOSTS), 0, COARSE)
    source = owner * COARSE + cell
    slot = jnp.arange(GHOSTS)
    box_ids = jnp.arange(BOXES)[None, :, None]
    side_face = jnp.clip((slot - 2 * XFACE_C) // SIDE_C, 0, 3)
    side_link = jnp.take(links, side_face, axis=1)[:, None, :]
    slot_b = slot[None, None, :]
    shared = jnp.where(slot_b < XFACE_C, box_ids > 0, jnp.where(slot_b < 2 * XFACE_C, box_ids < BOXES - 1, side_link >= 0))
    source = jnp.where(shared, -1, source)
    source = source.at[0, 0, 0].set(GROUPS * COARSE - 1)
    return source.astype(jnp.int32)


def draw_average_list(key, part):
    key = jax.random.fold_in(key, 23)

    def one_column(box_id):
        box_key = jax.random.fold_in(key, box_id)
        first_key, second_key, third_key = jax.random.split(box_key, 3)
        heavy = jax.random.randint(first_key, (), 0, GROUPS)
        heavy = jnp.where(box_id == 0, GROUPS - 1, jnp.where(box_id == BOXES - 1, 0, heavy))
        slots = jax.random.permutation(second_key, GROUPS * CBLK).astype(jnp.int32)
        ranking = jnp.where(slots // CBLK == heavy, 0, 1)
        chosen = slots[jnp.argsort(ranking, stable=True)][:GROUPS]
        return chosen[jax.random.permutation(third_key, GROUPS)]
    table = jax.vmap(one_column)(jnp.arange(BOXES))
    return jnp.transpose(table).astype(jnp.int32)


def draw_precond(key, part):
    key = jax.random.fold_in(key, 5)
    identity = (jnp.arange(S)[:, None] == jnp.arange(S)[None, :])[:, :, None, None]

    def one_group(group_id):
        group_key = jax.random.fold_in(key, group_id)
        first_key, second_key = jax.random.split(group_key)
        scale = jnp.exp(jax.random.uniform(first_key, (S, 1, BOXES * CX, FACE), jnp.float32, math.log(0.1), 0.0))
        noise = jnp.clip(jax.random.normal(second_key, (S, S, BOXES * CX, FACE), jnp.float32), -4.0, 4.0)
        return jnp.where(identity, scale, 0.1 * scale * noise).astype(jnp.bfloat16)
    stacked = lax.map(one_group, jnp.arange(GROUPS))
    return jnp.moveaxis(stacked, 0, 2)


def level_of(own_key, shape, cuts, low, largest):
    gain = 1.0
    for position, shards_of in cuts:
        steps = jax.random.uniform(jax.random.fold_in(jax.random.fold_in(own_key, 6), position), (shards_of,), jnp.float32, low / len(cuts), largest / len(cuts))
        gain = gain * jnp.repeat(jnp.exp(steps), shape[position] // shards_of).reshape((-1,) + (1,) * (len(shape) - 1 - position))
    return gain


def gaussian(own_key, dims, width, reach, cuts=(), kind=jnp.bfloat16):
    drawn = jax.random.normal(own_key, dims, jnp.float32) * width
    if len(cuts) > 0:
        drawn = level_of(own_key, dims, cuts, -0.22, 0.18) * drawn
    return jnp.clip(drawn, min=-reach, max=reach).astype(kind)


def setup_inputs(seed: int = 0) -> dict:
    arg_keys = jax.random.split(jax.random.key(seed), 11)
    return {
        "source_term": gaussian(arg_keys[0], (S, GROUPS, BOXES * CX, FACE), 4.0, 24.0, ((1, 32), (2, 8)), jnp.float32),
        "diffusion": jnp.clip(jnp.exp(jax.random.uniform(arg_keys[1], (S,), jnp.float32, math.log(0.1), math.log(2.0))), 0.1, 2.0),
        "stoich": gaussian(arg_keys[2], (S, R), R ** -0.5, 0.3125, (), jnp.float32),
        "orders": gaussian(arg_keys[3], (R, S), S ** -0.5, 0.875, (), jnp.float32),
        "rates": jnp.clip(jnp.exp(math.log(1.0) - 2.3025851 * jax.random.uniform(arg_keys[4], (R, GROUPS, BOXES * CX, FACE), jnp.float32) ** level_of(arg_keys[4], (R, GROUPS, BOXES * CX, FACE), ((1, 32), (2, 8)), -0.2, 0.2)), 0.1, 1.0),
        "precond": draw_precond(jax.random.fold_in(arg_keys[10], 71), 0),
        "coarse_field": gaussian(arg_keys[6], (S, GROUPS, BOXES * COARSE), 1.0, 6.0, ((1, 32), (2, 8)), jnp.float32),
        "neighbours": draw_neighbours(jax.random.fold_in(arg_keys[10], 71), 0),
        "ghost_list": draw_ghost_list(jax.random.fold_in(arg_keys[10], 71), 0),
        "average_list": draw_average_list(jax.random.fold_in(arg_keys[10], 71), 0),
    }


EXACT = lax.Precision.HIGHEST

def face_planes(core, side):
    return (core[..., :side], core[..., -side:], core[..., 0::side], core[..., side - 1::side])

def neighbour_sum(core, x_lower, x_upper, sides, side):
    padded = jnp.concatenate([x_lower[..., None, :], core, x_upper[..., None, :]], axis=-2)
    total = padded[..., :-2, :] + padded[..., 2:, :]
    total = total + jnp.concatenate([core[..., side:], sides[1]], axis=-1)
    total = total + jnp.concatenate([sides[0], core[..., :-side]], axis=-1)
    column = jnp.arange(core.shape[-1]) % side
    blank = jnp.zeros(core.shape[:-1] + (1,), core.dtype)
    ahead = jnp.concatenate([core[..., 1:], blank], axis=-1)
    behind = jnp.concatenate([blank, core[..., :-1]], axis=-1)
    total = total + jnp.where(column == side - 1, jnp.repeat(sides[3], side, axis=-1), ahead)
    total = total + jnp.where(column == 0, jnp.repeat(sides[2], side, axis=-1), behind)
    return total

def least_squares(columns, beta):
    count = len(columns)
    target = [beta] + [jnp.zeros_like(beta)] * count
    rotations = []
    upper = []
    for j in range(count):
        entries = list(columns[j])
        for i in range(j):
            cosine_part, sine_part = rotations[i]
            first = cosine_part * entries[i] + sine_part * entries[i + 1]
            second = cosine_part * entries[i + 1] - sine_part * entries[i]
            entries[i] = first
            entries[i + 1] = second
        radius = jnp.sqrt(entries[j] * entries[j] + entries[j + 1] * entries[j + 1])
        cosine_part = entries[j] / radius
        sine_part = entries[j + 1] / radius
        rotations.append((cosine_part, sine_part))
        entries[j] = radius
        target[j + 1] = -sine_part * target[j]
        target[j] = cosine_part * target[j]
        upper.append(entries[:j + 1])
    result = [None] * count
    for j in reversed(range(count)):
        running = target[j]
        for k in range(j + 1, count):
            running = running - upper[k][j] * result[k]
        result[j] = running / upper[j][j]
    return result

def reference(source_term, diffusion, stoich, orders, rates, precond, coarse_field, neighbours, ghost_list, average_list):
    shape = (S, GROUPS, BOXES, CX, FACE)
    half = FS // 2
    diffuse = diffusion[:, None, None, None, None]
    face_ids = jnp.arange(FACE)
    x_index = face_ids // FS // 2 * half + face_ids % FS // 2
    side_ids = jnp.arange(CX * FS)
    side_index = (side_ids // FS // 2 * half + side_ids % FS // 2).reshape(CX, FS)
    flat_coarse = coarse_field.reshape(S, GROUPS * BOXES * COARSE)
    owner = ghost_list // COARSE
    cell = ghost_list % COARSE
    box_ids = jnp.arange(BOXES)[None, :, None]
    location = jnp.where(ghost_list >= 0, owner * (BOXES * COARSE) + box_ids * COARSE + cell, 0).astype(jnp.int32)
    values = jnp.where(ghost_list[None] >= 0, jnp.take(flat_coarse, location, axis=1), 0.0)
    lower_x = values[..., :XFACE_C][..., x_index]
    upper_x = values[..., XFACE_C:2 * XFACE_C][..., x_index]
    sides = tuple((values[..., 2 * XFACE_C + f * SIDE_C:2 * XFACE_C + (f + 1) * SIDE_C][..., side_index] for f in range(4)))
    boundary = diffuse * neighbour_sum(jnp.zeros(shape, jnp.float32), lower_x, upper_x, sides, FS)
    right = source_term.reshape(shape) + boundary
    linked = neighbours >= 0
    partner = jnp.maximum(neighbours, 0).astype(jnp.int32)
    reaction = rates.reshape(R, -1)
    inverse = jnp.moveaxis(precond, 2, 0)

    def ghosts_of(field):
        planes = face_planes(field, FS)
        opposite = (planes[1], planes[0], planes[3], planes[2])
        return tuple((jnp.where(linked[None, :, f, None, None, None], jnp.take(opposite[f], partner[:, f], axis=1), 0.0) for f in range(4)))

    def operate(field):
        blank = jnp.zeros((S, GROUPS, 1, FACE), jnp.float32)
        x_low = jnp.concatenate([blank, field[:, :, :-1, -1]], axis=2)
        x_high = jnp.concatenate([field[:, :, 1:, 0], blank], axis=2)
        beside_all = neighbour_sum(field, x_low, x_high, ghosts_of(field), FS)
        progress = jnp.dot(orders, field.reshape(S, -1), precision=EXACT)
        chemistry = jnp.dot(stoich, reaction * progress, precision=EXACT).reshape(shape)
        return field + diffuse * (6.0 * field - beside_all) - chemistry

    def apply_block(pair):
        matrix, vector = pair
        return jnp.einsum('ijxc,jxc->ixc', matrix.astype(jnp.float32), vector, precision=EXACT)

    def precondition(field):
        moved = jnp.moveaxis(field.reshape(S, GROUPS, BOXES * CX, FACE), 1, 0)
        result = lax.map(apply_block, (inverse, moved))
        return jnp.moveaxis(result, 0, 1).reshape(shape)
    beta = jnp.sqrt(jnp.sum(right * right))
    basis = [right / beta]
    directions = []
    columns = []
    for j in range(ITERS):
        direction = precondition(basis[j])
        directions.append(direction)
        image = operate(direction)
        summed = jnp.stack([jnp.sum(basis[i] * image) for i in range(j + 1)])
        heights = [summed[i] for i in range(j + 1)]
        for i in range(j + 1):
            image = image - heights[i] * basis[i]
        length = jnp.sqrt(jnp.sum(image * image))
        columns.append(heights + [length])
        if j + 1 < ITERS:
            basis.append(image / length)
    weights = least_squares(columns, beta)
    correction = sum((weights[j] * directions[j] for j in range(ITERS)))
    pieces = correction.reshape(S, GROUPS, BOXES, CX // 2, 2, half, 2, half, 2)
    averaged = (lax.optimization_barrier(jnp.sum(pieces, axis=(4, 6, 8))) * 0.125).reshape(S, GROUPS, BOXES, BLOCK_C)
    blocks = coarse_field.reshape(S, GROUPS, BOXES, CBLK, BLOCK_C).transpose(0, 1, 3, 2, 4)
    blocks = blocks.reshape(S, GROUPS * CBLK, BOXES, BLOCK_C)
    box_grid = jnp.broadcast_to(jnp.arange(BOXES, dtype=jnp.int32)[None, :], (GROUPS, BOXES))
    blocks = blocks.at[:, average_list, box_grid].set(averaged)
    updated = blocks.reshape(S, GROUPS, CBLK, BOXES, BLOCK_C).transpose(0, 1, 3, 2, 4).reshape(S, GROUPS, BOXES * COARSE)
    return (correction.reshape(S, GROUPS, BOXES * CX, FACE), updated)
```

```python
import functools

import jax
import jax.numpy as jnp
import numpy as np
from jax import lax
from jax.experimental import pallas as pl
from jax.experimental.pallas import tpu as pltpu
from jax.sharding import PartitionSpec as P

FS = 16
ITERS = 4
SHIFT = 1.0
HALF = FS // 2
FACE = FS * FS
PAD = 56
ROWS = 2 * PAD
EXACT = lax.Precision.HIGHEST
VMEM = pl.BlockSpec(memory_space=pltpu.VMEM)
SMEM = pl.BlockSpec(memory_space=pltpu.SMEM)

NN = (((1,), (0,)), ((), ()))
NT = (((1,), (1,)), ((), ()))
TN = (((0,), (0,)), ((), ()))


def mm(a, b, dims=NN):
    return lax.dot_general(a, b, dims, precision=EXACT, preferred_element_type=jnp.float32)


def constants():
    cell = np.arange(FACE)
    y, z = cell // FS, cell % FS
    t = np.arange(FS)
    faces = np.zeros((4 * FS, FACE), np.float32)
    for f, lanes in enumerate((t, FACE - FS + t, t * FS, t * FS + FS - 1)):
        faces[f * FS + t, lanes] = 1.0
    inside = np.zeros((FACE, FACE), np.float32)
    for dy, dz in ((1, 0), (-1, 0), (0, 1), (0, -1)):
        ok = (y + dy >= 0) & (y + dy < FS) & (z + dz >= 0) & (z + dz < FS)
        inside[cell[ok], (y + dy)[ok] * FS + (z + dz)[ok]] = 1.0
    coarse = y // 2 * HALF + z // 2
    upsample = np.zeros((HALF * HALF, FACE), np.float32)
    upsample[coarse, cell] = 1.0
    side = np.zeros((4 * HALF, FACE), np.float32)
    for f in range(4):
        for k in range(FS):
            side[f * HALF + k // 2] += faces[f * FS + k]
    spread = np.zeros((2, 128, FACE), np.float32)
    spread[0, :64] = upsample
    spread[1, 64:96] = side
    halves = np.zeros((2, 128, FACE), np.float32)
    for m in range(4):
        c = np.arange(32)
        halves[0, 32 * m + c, 64 * m + c] = 1.0
        halves[1, 32 * m + c, 64 * m + 32 + c] = 1.0
    return faces, inside, upsample * 0.125, spread, halves


FACES, INSIDE, AVERAGE, SPREAD, HALVES = constants()


def call(kernel, name, shapes, args, specs, scratch=()):
    return pl.pallas_call(
        kernel,
        out_shape=[jax.ShapeDtypeStruct(s, jnp.float32) for s in shapes],
        in_specs=specs,
        out_specs=[VMEM] * len(shapes),
        scratch_shapes=list(scratch),
        compiler_params=pltpu.CompilerParams(vmem_limit_bytes=24 << 20),
        name=name,
    )(*args)


def gather_kernel(patch, entries, out):
    p = patch[...]
    p = jnp.concatenate([p, jnp.zeros((PAD - p.shape[0], FACE), jnp.float32)], axis=0)
    high = p.astype(jnp.bfloat16)
    rest = p - high.astype(jnp.float32)
    mid = rest.astype(jnp.bfloat16)
    low = (rest - mid.astype(jnp.float32)).astype(jnp.bfloat16)
    parts = jnp.concatenate([high, mid, low], axis=0)
    cell = lax.broadcasted_iota(jnp.int32, (FACE, 128), 0)
    for g in range(out.shape[0]):
        hot = (cell == entries[g : g + 1, :]).astype(jnp.float32).astype(jnp.bfloat16)
        got = jnp.dot(parts, hot, preferred_element_type=jnp.float32)
        out[g] = got[:PAD] + got[PAD : 2 * PAD] + got[2 * PAD :]


def mix(a, b, keep, shift):
    return jnp.where(keep, a, b) + pltpu.roll(jnp.where(keep, b, a), shift, 0)


def apply_inverse(inv, rows, u):
    count, depth = inv.shape[0], inv.shape[1]
    full = depth // 8
    for half in range(2):
        lanes = slice(128 * half, 128 * half + 128)
        row = lax.broadcasted_iota(jnp.int32, (8, 128), 0)
        bit2, bit1, bit0 = (row & 4) == 0, (row & 2) == 0, (row & 1) == 0
        w = [rows[half, 8 * k : 8 * k + 8, :] for k in range(full + 1)]
        zero = jnp.zeros((8, 128), jnp.float32)

        def one(i):
            if i >= count:
                return zero
            m = inv[i, :, lanes].astype(jnp.float32)
            total = m[0:8] * w[0]
            for k in range(1, full):
                total = total + m[8 * k : 8 * k + 8] * w[k]
            last = m[8 * full : depth]
            last = jnp.concatenate([last, jnp.zeros((8 - last.shape[0], 128), jnp.float32)], axis=0)
            return total + last * w[full]

        for block in range(PAD // 8):
            a = [one(8 * block + d) for d in range(8)]
            b = [mix(a[d], a[d + 2], bit1, 6) for d in (0, 1, 4, 5)]
            c = [mix(b[d], b[d + 2], bit2, 4) for d in range(2)]
            u[8 * block : 8 * block + 8, lanes] = jnp.where(bit0, c[0], pltpu.roll(c[1], 1, 0))
            u[PAD + 8 * block : PAD + 8 * block + 8, lanes] = jnp.where(
                bit0, pltpu.roll(c[0], 7, 0), c[1]
            )


def interleave(rows, field):
    for half in range(2):
        lanes = slice(128 * half, 128 * half + 128)
        rows.at[half][pl.ds(0, PAD, stride=2), :] = field[:PAD, lanes]
        rows.at[half][pl.ds(1, PAD, stride=2), :] = field[PAD:, lanes]


def separate(rows):
    planes = [
        jnp.concatenate([rows.at[h][pl.ds(x, PAD, stride=2), :] for h in range(2)], axis=1)
        for x in range(2)
    ]
    return jnp.concatenate(planes, axis=0)


def precondition(meta, inv, faces, w, rows, u, slots):
    interleave(rows, w)
    apply_inverse(inv, rows, u)
    planes = mm(faces[...], u[...], NT)
    for f in range(4):
        slots[meta[f], :, 0:ROWS] = planes[FS * f : FS * f + FS]


def first_kernel(meta, received, source, scale, spread, faces, inv, w_out, u, slots, rows):
    values = received[0]
    for g in range(1, received.shape[0]):
        values = values + received[g]
    beside = mm(values, spread[1])
    across = mm(values, spread[0])
    box = jnp.full((1, 1), meta[9], jnp.int32)
    lower = beside + jnp.where(box == 0, across, 0.0)
    upper = beside + jnp.where(box == meta[10], across, 0.0)
    boundary = jnp.concatenate([lower, upper], axis=0)
    species = source.shape[0]
    for half in range(2):
        rows[half, 0:species, :] = source[:, 128 * half : 128 * half + 128]
        rows[half, species:ROWS, :] = jnp.zeros((ROWS - species, 128), jnp.float32)
    right = separate(rows) + scale[:, 3:4] * boundary
    w_out[...] = right
    precondition(meta, inv, faces, right, rows, u, slots)


def operate(meta, received, low, high, u, w, scale, inside, faces, orders, stoich, rates):
    field = u[...]
    ghosts = []
    for f in range(4):
        plane = received[meta[f], :, 0:ROWS]
        ghosts.append(jnp.where(jnp.full((1, 1), meta[11 + f], jnp.int32) > 0, plane, 0.0))
    total = mm(field, inside[...]) + mm(jnp.concatenate(ghosts, axis=0), faces[...], TN)
    total = total + jnp.concatenate([low[...] + field[PAD:], field[:PAD] + high[...]], axis=0)
    both = jnp.concatenate([field[:PAD], field[PAD:]], axis=1)
    progress = mm(orders[...], both) * rates[...]
    chemistry = mm(stoich[...], progress)
    chemistry = jnp.concatenate([chemistry[:, :FACE], chemistry[:, FACE:]], axis=0)
    return scale[:, 0:1] * field - scale[:, 1:2] * total - chemistry - scale[:, 2:3] * w[...]


def step_kernel(meta, received, low, high, u, w, scale, inside, faces, orders, stoich, rates, inv, w_out, u_out, slots, rows):
    image = operate(meta, received, low, high, u, w, scale, inside, faces, orders, stoich, rates)
    w_out[...] = image
    precondition(meta, inv, faces, image, rows, u_out, slots)


def last_kernel(meta, received, low, high, u, w0, w1, w2, w3, scale, inside, faces, orders, stoich, rates, out):
    image = operate(meta, received, low, high, u, w3, scale, inside, faces, orders, stoich, rates)
    w = [w0[...], w1[...], w2[...], w3[...], image]
    lane = lax.broadcasted_iota(jnp.int32, (1, 128), 1)
    line = jnp.zeros((1, 128), jnp.float32)
    k = 0
    for a in range(ITERS + 1):
        for b in range(a + 1):
            part = jnp.sum(w[a] * w[b], axis=0, keepdims=True)
            part = jnp.sum(part, axis=1, keepdims=True)
            line = jnp.where(lane == k, part, line)
            k += 1
    out[...] = jnp.broadcast_to(line, out.shape)


def solve(gram, shift):
    def g(a, b):
        return gram[(max(a, b), min(a, b))]

    n = ITERS
    target = [g(a + 1, 0) + shift * g(a, 0) for a in range(n)]
    normal = {}
    for a in range(n):
        for b in range(a + 1):
            normal[a, b] = (
                g(a + 1, b + 1) + shift * (g(a + 1, b) + g(a, b + 1)) + shift * shift * g(a, b)
            )
    size = [lax.rsqrt(normal[a, a]) for a in range(n)]
    target = [target[a] * size[a] for a in range(n)]
    lower = {}
    inverse = [None] * n
    for a in range(n):
        for b in range(a + 1):
            value = normal[a, b] * size[a] * size[b]
            for c in range(b):
                value = value - lower[a, c] * lower[b, c]
            if a == b:
                inverse[a] = lax.rsqrt(value)
            else:
                lower[a, b] = value * inverse[b]
    half = []
    for a in range(n):
        value = target[a]
        for c in range(a):
            value = value - lower[a, c] * half[c]
        half.append(value * inverse[a])
    result = [None] * n
    for a in reversed(range(n)):
        value = half[a]
        for c in range(a + 1, n):
            value = value - lower[c, a] * result[c]
        result[a] = value * inverse[a]
    return [result[a] * size[a] for a in range(n)]


def finish_kernel(meta, lines, u0, u1, u2, u3, scale, average, correction, slots, rows):
    line = jnp.sum(lines[...], axis=0, keepdims=True)
    gram = {}
    k = 0
    for a in range(ITERS + 1):
        for b in range(a + 1):
            gram[a, b] = line[:, k : k + 1]
            k += 1
    shift = scale[0:1, 2:3]
    weights = solve(gram, shift)
    factor = scale[0:1, 4:5]
    total = jnp.zeros((ROWS, FACE), jnp.float32)
    for weight, u in zip(weights, (u0, u1, u2, u3)):
        total = total + (weight * factor) * u[...]
    interleave(rows, total)
    for half in range(2):
        lanes = slice(128 * half, 128 * half + 128)
        correction[:, lanes] = rows[half, 0 : correction.shape[0], :]
    summed = total[:PAD] + total[PAD:]
    blank = jnp.zeros((64 - PAD, FACE), jnp.float32)
    spread = jnp.concatenate([summed, blank, summed, blank], axis=0)
    mean = mm(average[...], spread, NT)
    lane = lax.broadcasted_iota(jnp.int32, (32, 128), 1)
    slots[meta[4]] = jnp.where(lane < 64, mean[:32], mean[32:])


def update_kernel(meta, received, patch, halves, out):
    blocks = []
    lane = lax.broadcasted_iota(jnp.int32, (1, FACE), 1)
    covered = jnp.zeros((1, FACE), jnp.int32)
    for m in range(4):
        source = meta[5 + m]
        block = received[jnp.maximum(source, 0)]
        blocks.append(jnp.where(jnp.full((1, 1), source, jnp.int32) >= 0, block, 0.0))
        covered = jnp.where(lane // 64 == m, source, covered)
    stacked = jnp.concatenate(blocks, axis=0)
    species = patch.shape[0]
    first = mm(stacked, halves[0], TN)[0:species]
    second = mm(stacked, halves[1], TN)[64 : 64 + species]
    out[...] = jnp.where(covered >= 0, first + second, patch[...])


def on_device(
    source_term,
    diffusion,
    stoich,
    orders,
    rates,
    precond,
    coarse_field,
    neighbours,
    ghost_list,
    average_list,
):
    species, reactions = stoich.shape
    groups = lax.axis_size("grp")
    boxes = lax.axis_size("box")
    me = lax.axis_index("grp")
    box = lax.axis_index("box")
    f32 = jnp.float32

    links = lax.dynamic_index_in_dim(neighbours, me, 0, keepdims=False)
    owned = average_list[:, 0]
    wanted = me * 4 + jnp.arange(4)
    found = jnp.max(
        jnp.where(owned[None, :] == wanted[:, None], jnp.arange(groups)[None, :], -1), axis=1
    )
    home = lax.dynamic_index_in_dim(owned, me, 0, keepdims=True) // 4
    meta = jnp.concatenate(
        [
            jnp.where(links >= 0, links, me),
            home,
            found,
            jnp.stack([box, jnp.asarray(boxes - 1, box.dtype)]),
            (links >= 0).astype(jnp.int32),
            jnp.zeros((1,), jnp.int32),
        ]
    ).astype(jnp.int32)

    wide = 1.0 + 12.0 * jnp.max(diffusion)
    wide = wide + jnp.sqrt(jnp.sum(stoich * stoich)) * jnp.sqrt(jnp.sum(orders * orders))
    unit = 32.0 / wide
    column = jnp.pad(diffusion, (0, PAD - species))
    mask = (jnp.arange(PAD) < species).astype(f32)
    scale = jnp.stack(
        [
            unit * (1.0 + 6.0 * column) * mask,
            unit * column,
            jnp.full((PAD,), SHIFT, f32) * unit,
            column,
            jnp.full((PAD,), 1.0, f32) * unit,
        ],
        axis=1,
    )
    scale = jnp.concatenate([scale, scale], axis=0)
    stoich_s = jnp.pad(stoich * unit, ((0, PAD - species), (0, 0)))
    orders_s = jnp.pad(orders, ((0, 0), (0, PAD - species)))
    rates_s = rates.reshape(reactions, 2 * FACE)
    inverse = precond.reshape(species, 2 * species, FACE)
    source = source_term.reshape(2 * species, FACE)
    patch = coarse_field.reshape(species, FACE)

    lists = ghost_list[:, 0, :]
    entries = jnp.concatenate(
        [jnp.where(box == 0, lists[:, :64], lists[:, 64:128]), lists[:, 128:]], axis=1
    )
    entries = jnp.where(entries >= 0, entries - me * FACE, -1)
    entries = jnp.pad(entries, ((0, 0), (0, 128 - entries.shape[1])), constant_values=-1)

    def exchange(slots):
        return lax.all_to_all(slots, "grp", 0, 0, tiled=True)

    (asked,) = call(gather_kernel, "gather", [(groups, PAD, 128)], (patch, entries), [VMEM] * 2)
    received = exchange(asked)
    faces = jnp.asarray(FACES)
    inside = jnp.asarray(INSIDE)
    outs = [(ROWS, FACE), (ROWS, FACE), (groups, FS, 128)]
    rows = [pltpu.VMEM((2, ROWS, 128), f32)]
    w, u, slots = call(
        first_kernel,
        "first",
        outs,
        (meta, received, source, scale, jnp.asarray(SPREAD), faces, inverse),
        [SMEM] + [VMEM] * 6,
        rows,
    )
    basis, directions = [w], [u]
    for j in range(ITERS):
        low = lax.ppermute(u[PAD:], "box", [(i, i + 1) for i in range(boxes - 1)])
        high = lax.ppermute(u[:PAD], "box", [(i + 1, i) for i in range(boxes - 1)])
        received = exchange(slots)
        shared = (scale, inside, faces, orders_s, stoich_s, rates_s)
        if j + 1 < ITERS:
            w, u, slots = call(
                step_kernel,
                "step%d" % j,
                outs,
                (meta, received, low, high, u, w) + shared + (inverse,),
                [SMEM] + [VMEM] * 12,
                rows,
            )
            basis.append(w)
            directions.append(u)
        else:
            (lines,) = call(
                last_kernel,
                "last",
                [(groups * boxes, 128)],
                (meta, received, low, high, u) + tuple(basis) + shared,
                [SMEM] + [VMEM] * 14,
            )
    lines = lax.all_to_all(lines, ("grp", "box"), 0, 0, tiled=True)
    correction, slots = call(
        finish_kernel,
        "finish",
        [(2 * species, FACE), (groups, 32, 128)],
        (meta, lines) + tuple(directions) + (scale, jnp.asarray(AVERAGE)),
        [SMEM] + [VMEM] * 7,
        rows,
    )
    received = exchange(slots)
    (updated,) = call(
        update_kernel,
        "update",
        [(species, FACE)],
        (meta, received, patch, jnp.asarray(HALVES)),
        [SMEM] + [VMEM] * 3,
    )
    return (
        correction.reshape(species, 1, 2, FACE),
        updated.reshape(species, 1, FACE),
    )


def solution(mesh):
    placed = (
        P(None, "grp", "box", None),
        P(),
        P(),
        P(),
        P(None, "grp", "box", None),
        P(None, None, "grp", "box", None),
        P(None, "grp", "box"),
        P(),
        P(None, "box", None),
        P(None, "box"),
    )
    return jax.shard_map(
        on_device,
        mesh=mesh,
        in_specs=placed,
        out_specs=(P(None, "grp", "box", None), P(None, "grp", "box")),
        check_vma=False,
    )
```

```python
import functools

import jax
import jax.numpy as jnp
import numpy as np
from jax import lax
from jax.experimental import pallas as pl
from jax.experimental.pallas import tpu as pltpu
from jax.sharding import PartitionSpec as P

FS = 16
ITERS = 4
SHIFT = 1.0
HALF = FS // 2
FACE = FS * FS
PAD = 56
ROWS = 2 * PAD
SLOT = 40
EXACT = lax.Precision.HIGHEST
VMEM = pl.BlockSpec(memory_space=pltpu.VMEM)
SMEM = pl.BlockSpec(memory_space=pltpu.SMEM)

NN = (((1,), (0,)), ((), ()))
NT = (((1,), (1,)), ((), ()))
TN = (((0,), (0,)), ((), ()))


def mm(a, b, dims=NN):
    return lax.dot_general(a, b, dims, precision=EXACT, preferred_element_type=jnp.float32)


def two(value):
    high = value.astype(jnp.bfloat16)
    return high, (value - high.astype(jnp.float32)).astype(jnp.bfloat16)


def select(a, b):
    parts = jnp.concatenate(two(a), axis=0)
    got = lax.dot_general(parts, b, NN, preferred_element_type=jnp.float32)
    return got[: a.shape[0]] + got[a.shape[0] :]


def constants():
    cell = np.arange(FACE)
    y, z = cell // FS, cell % FS
    t = np.arange(FS)
    faces = np.zeros((4 * FS, FACE), np.float32)
    for f, lanes in enumerate((t, FACE - FS + t, t * FS, t * FS + FS - 1)):
        faces[f * FS + t, lanes] = 1.0
    inside = np.zeros((FACE, FACE), np.float32)
    for dy, dz in ((1, 0), (-1, 0), (0, 1), (0, -1)):
        ok = (y + dy >= 0) & (y + dy < FS) & (z + dz >= 0) & (z + dz < FS)
        inside[cell[ok], (y + dy)[ok] * FS + (z + dz)[ok]] = 1.0
    coarse = y // 2 * HALF + z // 2
    upsample = np.zeros((HALF * HALF, FACE), np.float32)
    upsample[coarse, cell] = 1.0
    halves = np.zeros((128, 2 * FACE), np.float32)
    for m in range(4):
        c = np.arange(32)
        halves[32 * m + c, 64 * m + c] = 1.0
        halves[32 * m + c, FACE + 64 * m + 32 + c] = 1.0
    return faces, inside, upsample * 0.125, halves


FACES, INSIDE, AVERAGE, HALVES = constants()


def call(kernel, name, shapes, args, specs, scratch=(), out_specs=None):
    return pl.pallas_call(
        kernel,
        out_shape=[
            jax.ShapeDtypeStruct(s[:-1], s[-1])
            if not isinstance(s[-1], int)
            else jax.ShapeDtypeStruct(s, jnp.float32)
            for s in shapes
        ],
        in_specs=specs,
        out_specs=out_specs or [VMEM] * len(shapes),
        scratch_shapes=list(scratch),
        compiler_params=pltpu.CompilerParams(vmem_limit_bytes=24 << 20),
        name=name,
    )(*args)


def split(value):
    high = value.astype(jnp.bfloat16)
    rest = value - high.astype(jnp.float32)
    middle = rest.astype(jnp.bfloat16)
    low = (rest - middle.astype(jnp.float32)).astype(jnp.bfloat16)
    return high, middle, low


def gather_kernel(ids, patch, lists, out, hot):
    species = patch.shape[0]
    row = lax.broadcasted_iota(jnp.int32, (species, FACE), 0)
    lane = lax.broadcasted_iota(jnp.int32, (species, FACE), 1)
    place = ((lane == row) | (lane == row + 192)).astype(jnp.float32)
    turned = mm(patch[:, 0, :], place, TN)
    parts = jnp.concatenate(
        [jnp.concatenate(split(turned[:, 128 * h : 128 * h + 128]), axis=1) for h in range(2)],
        axis=0,
    )
    entries = lists[:, 0, :].astype(jnp.float32) - (ids[0] * FACE).astype(jnp.float32)
    across = entries[:, 0:128].T
    beside = entries[:, 128:160].T
    entries = jnp.concatenate(
        [
            jnp.maximum(across[0:64], across[64:128]),
            jnp.maximum(beside[0:8], beside[8:16]),
            jnp.maximum(beside[16:24], beside[24:32]),
        ],
        axis=0,
    )
    cell = lax.broadcasted_iota(jnp.int32, (SLOT, FACE), 1).astype(jnp.float32)
    groups = out.shape[0]
    for g in range(0, groups, 2):
        pair = [
            jnp.concatenate(
                [
                    (cell == entries[SLOT * h : SLOT * h + SLOT, k : k + 1]).astype(jnp.float32)
                    for h in range(2)
                ],
                axis=1,
            )
            for k in (g, g + 1)
        ]
        hot[SLOT * g : SLOT * g + 2 * SLOT, :] = jnp.concatenate(pair, axis=0).astype(jnp.bfloat16)
    step = 8
    for g in range(0, groups, step):
        got = jnp.dot(
            hot[SLOT * g : SLOT * (g + step), :], parts, preferred_element_type=jnp.float32
        )
        got = got[:, 0:128] + got[:, 128:256] + got[:, 256:384]
        for k in range(step):
            out[g + k] = got[SLOT * k : SLOT * k + SLOT]


def prepare_kernel(ids, owned, diffusion, stoich, orders, scale, stoich_out, orders_out, sources):
    me = ids[0]
    found = [jnp.int32(-1)] * 4
    for g in range(owned.shape[1]):
        entry = owned[0, g]
        found = [jnp.where(entry == me * 4 + m, g, found[m]) for m in range(4)]
    for m in range(4):
        sources[m] = found[m]
    d = diffusion[...]
    species = d.shape[0]
    column = jnp.concatenate([d, jnp.zeros((PAD - species, 1), jnp.float32)], axis=0)

    def total(value):
        return jnp.sum(jnp.sum(value, axis=0, keepdims=True), axis=1, keepdims=True)

    wide = 1.0 + 12.0 * jnp.max(column, axis=0, keepdims=True)
    s, o = stoich[...], orders[...]
    wide = wide + jnp.sqrt(total(s * s)) * jnp.sqrt(total(o * o))
    unit = 32.0 / wide
    reactions = s.shape[1]
    high, low = two(jnp.concatenate([s * unit, jnp.zeros((PAD - species, reactions))], axis=0))
    stoich_out[...] = jnp.concatenate([high, low], axis=0)
    o = jnp.concatenate([o, jnp.zeros((PAD - species, reactions))], axis=0).T
    high, low = two(o)
    orders_out[...] = jnp.concatenate([high, high, low], axis=1)
    lane = lax.broadcasted_iota(jnp.int32, (PAD, 128), 1)
    row = lax.broadcasted_iota(jnp.int32, (PAD, 1), 0)
    diagonal = jnp.where(row < species, unit * (1.0 + 6.0 * column), 0.0)
    value = jnp.where(lane == 0, diagonal, 0.0)
    value = jnp.where(lane == 1, unit * column, value)
    value = jnp.where(lane == 2, SHIFT * unit, value)
    value = jnp.where(lane == 3, column, value)
    value = jnp.where(lane == 4, unit, value)
    scale[0:PAD, :] = value
    scale[PAD:, :] = value


def mix(a, b, keep, shift):
    return jnp.where(keep, a, b) + pltpu.roll(jnp.where(keep, b, a), shift, 0)


def apply_inverse(inv, rows, u):
    count, depth = inv.shape[0], inv.shape[1]
    full = depth // 8
    for half in range(2):
        lanes = slice(128 * half, 128 * half + 128)
        row = lax.broadcasted_iota(jnp.int32, (8, 128), 0)
        bit2, bit1, bit0 = (row & 4) == 0, (row & 2) == 0, (row & 1) == 0
        w = [rows[half, 8 * k : 8 * k + 8, :] for k in range(full + 1)]
        zero = jnp.zeros((8, 128), jnp.float32)

        def one(i):
            if i >= count:
                return zero
            m = inv[i, :, lanes].astype(jnp.float32)
            total = m[0:8] * w[0]
            for k in range(1, full):
                total = total + m[8 * k : 8 * k + 8] * w[k]
            last = m[8 * full : depth]
            last = jnp.concatenate([last, jnp.zeros((8 - last.shape[0], 128), jnp.float32)], axis=0)
            return total + last * w[full]

        for block in range(PAD // 8):
            a = [one(8 * block + d) for d in range(8)]
            b = [mix(a[d], a[d + 2], bit1, 6) for d in (0, 1, 4, 5)]
            c = [mix(b[d], b[d + 2], bit2, 4) for d in range(2)]
            u[8 * block : 8 * block + 8, lanes] = jnp.where(bit0, c[0], pltpu.roll(c[1], 1, 0))
            u[PAD + 8 * block : PAD + 8 * block + 8, lanes] = jnp.where(
                bit0, pltpu.roll(c[0], 7, 0), c[1]
            )


def interleave(rows, field):
    for half in range(2):
        lanes = slice(128 * half, 128 * half + 128)
        rows.at[half][pl.ds(0, PAD, stride=2), :] = field[:PAD, lanes]
        rows.at[half][pl.ds(1, PAD, stride=2), :] = field[PAD:, lanes]


def separate(rows):
    planes = [
        jnp.concatenate([rows.at[h][pl.ds(x, PAD, stride=2), :] for h in range(2)], axis=1)
        for x in range(2)
    ]
    return jnp.concatenate(planes, axis=0)


def flag(condition):
    return jnp.full((1, 1), condition, jnp.int32) != 0


def precondition(ids, inv, w, rows, u, near, far):
    interleave(rows, w)
    apply_inverse(inv, rows, u)

    @pl.when(ids[1] % 2 == 0)
    def _():
        near[...] = u[PAD:]
        far[...] = u[:PAD]

    @pl.when(ids[1] % 2 == 1)
    def _():
        near[...] = u[:PAD]
        far[...] = u[PAD:]


def first_kernel(ids, links, received, source, scale, inv, w_out, near, far, u, rows):
    values = received[0]
    for g in range(1, received.shape[0]):
        values = values + received[g]
    me = ids[0]
    row = lax.broadcasted_iota(jnp.int32, (SLOT, FACE), 0)
    cell = lax.broadcasted_iota(jnp.int32, (SLOT, FACE), 1)
    y, z = cell // FS, cell % FS
    coarse = y // 2 * HALF + z // 2
    first = 64 - SLOT
    y_face = jnp.where(links[0, me] < 0, 0, FS - 1)
    z_face = jnp.where(links[2, me] < 0, 0, FS - 1)
    sides = ((y == y_face) & (row == first + z // 2)).astype(jnp.float32)
    sides = sides + ((z == z_face) & (row == first + HALF + y // 2)).astype(jnp.float32)
    faces = [coarse == row, (coarse == row + SLOT) & (row < first)]
    faces = [face.astype(jnp.float32) for face in faces]
    across = mm(values, jnp.concatenate([faces[0], faces[1], sides], axis=1), TN)
    beside = across[64 : 64 + PAD, 2 * FACE :]
    across = across[0:PAD, :FACE] + across[64 : 64 + PAD, FACE : 2 * FACE]
    bottom = flag(ids[1] == 0)
    boundary = jnp.concatenate(
        [beside + jnp.where(bottom, across, 0.0), beside + jnp.where(bottom, 0.0, across)], axis=0
    )
    species = source.shape[0]
    for half in range(2):
        rows[half, 0:species, :] = source[:, 128 * half : 128 * half + 128]
        rows[half, species:ROWS, :] = jnp.zeros((ROWS - species, 128), jnp.float32)
    right = separate(rows) + scale[:, 3:4] * boundary
    w_out[...] = right
    precondition(ids, inv, right, rows, u, near, far)


def dots(vectors, last, line):
    lane = lax.broadcasted_iota(jnp.int32, (1, 128), 1)
    count = len(vectors)
    for b, vector in enumerate(vectors + [last]):
        part = jnp.sum(last * vector, axis=0, keepdims=True)
        part = jnp.sum(part, axis=1, keepdims=True)
        line = jnp.where(lane == count * (count + 1) // 2 + b, part, line)
    return line


def local_kernel(j, ids, links, *refs):
    u, scale, inside, faces, orders, stoich, rates = refs[:7]
    basis = refs[7 : 8 + j]
    part, slots, line_out = refs[-3:]
    line = refs[8 + j][...] if j else jnp.zeros((1, 128), jnp.float32)
    me = ids[0]
    field = u[...]
    lower, upper = field[:PAD], field[PAD:]
    face = faces[...].astype(jnp.bfloat16)
    planes = lax.dot_general(
        jnp.concatenate([face, face], axis=1),
        jnp.concatenate(two(field), axis=1),
        NT,
        preferred_element_type=jnp.float32,
    )
    for f in range(4):
        other = links[f, me]
        slots[jnp.where(other < 0, me, other), :, 0:ROWS] = planes[FS * f : FS * f + FS]
    total = select(field, inside[...].astype(jnp.bfloat16))
    total = total + jnp.concatenate([field[PAD:], field[:PAD]], axis=0)
    both = jnp.concatenate([lower, upper], axis=1)
    high, low = two(both)
    progress = jnp.dot(
        orders[...], jnp.concatenate([high, low, high], axis=0), preferred_element_type=jnp.float32
    )
    high, low = two(progress * rates[...])
    chemistry = jnp.dot(stoich[...], high, preferred_element_type=jnp.float32)
    chemistry = chemistry[:PAD] + chemistry[PAD:]
    chemistry = chemistry + jnp.dot(stoich[:PAD, :], low, preferred_element_type=jnp.float32)
    chemistry = jnp.concatenate([chemistry[:, :FACE], chemistry[:, FACE:]], axis=0)
    w = basis[-1][...]
    part[...] = scale[:, 0:1] * field - scale[:, 1:2] * total - chemistry - scale[:, 2:3] * w
    line_out[...] = dots([ref[...] for ref in basis[:-1]], w, line)


def image_of(ids, links, received, near, far, part, scale, faces):
    me = ids[0]
    even = (ids[1] % 2 == 0).astype(jnp.float32)
    end = jnp.logical_or(ids[1] == 0, ids[1] == ids[2])
    live = jnp.where(end, 0.0, 1.0)
    low = (1.0 - even) * near[...] + (even * live) * far[...]
    high = even * near[...] + ((1.0 - even) * live) * far[...]
    ghosts = []
    for f in range(4):
        other = links[f, me]
        plane = received[jnp.where(other < 0, me, other), :, 0:ROWS]
        ghosts.append(jnp.where(other < 0, 0.0, 1.0) * plane)
    face = faces[...].astype(jnp.bfloat16)
    total = lax.dot_general(
        jnp.concatenate(two(jnp.concatenate(ghosts, axis=0)), axis=0),
        jnp.concatenate([face, face], axis=0),
        TN,
        preferred_element_type=jnp.float32,
    )
    total = total + jnp.concatenate([low, high], axis=0)
    return part[...] - scale[:, 1:2] * total


def combine_kernel(ids, links, received, near_in, far_in, part, scale, faces, inv, w_out, near, far, u, rows):
    image = image_of(ids, links, received, near_in, far_in, part, scale, faces)
    w_out[...] = image
    precondition(ids, inv, image, rows, u, near, far)


def last_kernel(ids, links, received, near, far, part, scale, faces, w0, w1, w2, w3, line, out):
    image = image_of(ids, links, received, near, far, part, scale, faces)
    result = dots([w0[...], w1[...], w2[...], w3[...]], image, line[...])
    out[...] = jnp.broadcast_to(result, out.shape)


def solve(gram, shift):
    def g(a, b):
        return gram[(max(a, b), min(a, b))]

    n = ITERS
    target = [g(a + 1, 0) + shift * g(a, 0) for a in range(n)]
    normal = {}
    for a in range(n):
        for b in range(a + 1):
            normal[a, b] = (
                g(a + 1, b + 1) + shift * (g(a + 1, b) + g(a, b + 1)) + shift * shift * g(a, b)
            )
    size = [lax.rsqrt(normal[a, a]) for a in range(n)]
    target = [target[a] * size[a] for a in range(n)]
    lower = {}
    inverse = [None] * n
    for a in range(n):
        for b in range(a + 1):
            value = normal[a, b] * size[a] * size[b]
            for c in range(b):
                value = value - lower[a, c] * lower[b, c]
            if a == b:
                inverse[a] = lax.rsqrt(value)
            else:
                lower[a, b] = value * inverse[b]
    half = []
    for a in range(n):
        value = target[a]
        for c in range(a):
            value = value - lower[a, c] * half[c]
        half.append(value * inverse[a])
    result = [None] * n
    for a in reversed(range(n)):
        value = half[a]
        for c in range(a + 1, n):
            value = value - lower[c, a] * result[c]
        result[a] = value * inverse[a]
    return [result[a] * size[a] for a in range(n)]


def finish_kernel(ids, owned, lines, *refs):
    fields = refs[:ITERS]
    scale, average, correction, slots, rows = refs[ITERS:]
    line = jnp.sum(lines[...], axis=0, keepdims=True)
    gram = {}
    k = 0
    for a in range(ITERS + 1):
        for b in range(a + 1):
            gram[a, b] = line[:, k : k + 1]
            k += 1
    weights = solve(gram, scale[0:1, 2:3])
    factor = scale[0:1, 4:5]
    total = (weights[0] * factor) * fields[0][...]
    for weight, field in zip(weights[1:], fields[1:]):
        total = total + (weight * factor) * field[...]
    interleave(rows, total)
    for half in range(2):
        lanes = slice(128 * half, 128 * half + 128)
        correction[:, lanes] = rows[half, 0 : correction.shape[0], :]
    summed = total[:PAD] + total[PAD:]
    blank = jnp.zeros((64 - PAD, FACE), jnp.float32)
    spread = jnp.concatenate([summed, blank, summed, blank], axis=0)
    weight = average[...].astype(jnp.bfloat16)
    mean = lax.dot_general(
        jnp.concatenate([weight, weight], axis=1),
        jnp.concatenate(two(spread), axis=1),
        NT,
        preferred_element_type=jnp.float32,
    )
    lane = lax.broadcasted_iota(jnp.int32, (32, 128), 1)
    slots[owned[0, ids[0]] // 4] = jnp.where(lane < 64, mean[:32], mean[32:])


def update_kernel(sources, received, patch, halves, out, stacked):
    lane = lax.broadcasted_iota(jnp.int32, (1, FACE), 1)
    covered = jnp.zeros((1, FACE), jnp.int32)
    for m in range(4):
        source = sources[m]
        here = slice(32 * m, 32 * m + 32)

        @pl.when(source >= 0)
        def _():
            stacked[here, :] = received[source]

        @pl.when(source < 0)
        def _():
            stacked[here, :] = jnp.zeros((32, 128), jnp.float32)

        covered = jnp.where(lane // 64 == m, source, covered)
    species = patch.shape[0]
    half = halves[...].astype(jnp.bfloat16)
    got = lax.dot_general(
        jnp.concatenate(two(stacked[...]), axis=0),
        jnp.concatenate([half, half], axis=0),
        TN,
        preferred_element_type=jnp.float32,
    )
    got = got[0:species, :FACE] + got[64 : 64 + species, FACE:]
    out[:, 0, :] = jnp.where(covered >= 0, got, patch[...])


def on_device(
    source_term,
    diffusion,
    stoich,
    orders,
    rates,
    precond,
    coarse_field,
    neighbours,
    ghost_list,
    average_list,
):
    species, reactions = stoich.shape
    groups = lax.axis_size("grp")
    boxes = lax.axis_size("box")
    me = lax.axis_index("grp")
    box = lax.axis_index("box")
    f32 = jnp.float32
    barrier = lax.optimization_barrier

    ids = jnp.stack([me, box, jnp.asarray(boxes - 1, box.dtype)]).astype(jnp.int32)
    links = neighbours.T
    owned = average_list.T
    even_swap = [(i, i ^ 1) for i in range(boxes)]
    odd_swap = [(i, (i + (1 if i % 2 else -1)) % boxes) for i in range(boxes)]

    def exchange(slots):
        return lax.all_to_all(slots, "grp", 0, 0, tiled=True)

    (asked,) = call(
        gather_kernel, "gather", [(groups, SLOT, 128)], (ids, coarse_field, ghost_list), [SMEM] + [VMEM] * 2,
        [pltpu.VMEM((groups * SLOT, 2 * FACE), jnp.bfloat16)],
    )
    received = exchange(asked)
    scale, stoich_s, orders_s, sources = call(
        prepare_kernel,
        "prepare",
        [(ROWS, 128), (2 * PAD, reactions, jnp.bfloat16), (reactions, 3 * PAD, jnp.bfloat16), (4, jnp.int32)],
        (ids, owned, diffusion.reshape(species, 1), stoich, orders.T),
        [SMEM] * 2 + [VMEM] * 3,
        (),
        [VMEM] * 3 + [SMEM],
    )
    rates_s = rates.reshape(reactions, 2 * FACE)
    inverse = precond.reshape(species, 2 * species, FACE)
    source = source_term.reshape(2 * species, FACE)
    faces = jnp.asarray(FACES)
    inside = jnp.asarray(INSIDE)
    outs = [(ROWS, FACE), (PAD, FACE), (PAD, FACE), (ROWS, FACE)]
    rows = [pltpu.VMEM((2, ROWS, 128), f32)]
    w, near, far, u = call(
        first_kernel,
        "first",
        outs,
        (ids, links, received, source, scale, inverse),
        [SMEM] * 2 + [VMEM] * 4,
        rows,
    )
    basis, directions = [w], [u]
    line = ()
    for j in range(ITERS):
        near_in = lax.ppermute(near, "box", even_swap)
        far_in = lax.ppermute(far, "box", odd_swap)
        part, slots, line = call(
            functools.partial(local_kernel, j),
            "local%d" % j,
            [(ROWS, FACE), (groups, FS, 128), (1, 128)],
            (ids, links, u, scale, inside, faces, orders_s, stoich_s, rates_s)
            + tuple(basis)
            + ((line,) if j else ()),
            [SMEM] * 2 + [VMEM] * (9 + j if j else 8),
        )
        slots, near_in, far_in, part, line = barrier((slots, near_in, far_in, part, line))
        received = exchange(slots)
        received, near_in, far_in, part, line = barrier((received, near_in, far_in, part, line))
        shared = (ids, links, received, near_in, far_in, part, scale, faces)
        if j + 1 < ITERS:
            w, near, far, u = call(
                combine_kernel,
                "combine%d" % j,
                outs,
                shared + (inverse,),
                [SMEM] * 2 + [VMEM] * 7,
                rows,
            )
            basis.append(w)
            directions.append(u)
        else:
            (lines,) = call(
                last_kernel,
                "last",
                [(groups * boxes, 128)],
                shared + tuple(basis) + (line,),
                [SMEM] * 2 + [VMEM] * 11,
            )
    lines = lax.all_to_all(lines, ("grp", "box"), 0, 0, tiled=True)
    correction, slots = call(
        finish_kernel,
        "finish",
        [(2 * species, FACE), (groups, 32, 128)],
        (ids, owned, lines) + tuple(directions) + (scale, jnp.asarray(AVERAGE)),
        [SMEM] * 2 + [VMEM] * 7,
        rows,
    )
    received = exchange(slots)
    (updated,) = call(
        update_kernel,
        "update",
        [(species, 1, FACE)],
        (sources, received, coarse_field.reshape(species, FACE), jnp.asarray(HALVES)),
        [SMEM] + [VMEM] * 3,
        [pltpu.VMEM((128, 128), f32)],
    )
    return correction.reshape(species, 1, 2, FACE), updated


def solution(mesh):
    placed = (
        P(None, "grp", "box", None),
        P(),
        P(),
        P(),
        P(None, "grp", "box", None),
        P(None, None, "grp", "box", None),
        P(None, "grp", "box"),
        P(),
        P(None, "box", None),
        P(None, "box"),
    )
    return jax.shard_map(
        on_device,
        mesh=mesh,
        in_specs=placed,
        out_specs=(P(None, "grp", "box", None), P(None, "grp", "box")),
        check_vma=False,
    )
```

```python
import functools

import jax
import jax.numpy as jnp
import numpy as np
from jax import lax
from jax.experimental import pallas as pl
from jax.experimental.pallas import tpu as pltpu
from jax.sharding import PartitionSpec as P

FS = 16
ITERS = 4
SHIFT = 1.0
HALF = FS // 2
FACE = FS * FS
PAD = 56
ROWS = 2 * PAD
SLOT = 40
WHOLE = 66900000
EXACT = lax.Precision.HIGHEST
HBM = pl.BlockSpec(memory_space=pltpu.HBM)
VMEM = pl.BlockSpec(memory_space=pltpu.VMEM)
SMEM = pl.BlockSpec(memory_space=pltpu.SMEM)

NN = (((1,), (0,)), ((), ()))
NT = (((1,), (1,)), ((), ()))
TN = (((0,), (0,)), ((), ()))


def mm(a, b, dims=NN):
    return lax.dot_general(a, b, dims, precision=EXACT, preferred_element_type=jnp.float32)


def two(value):
    high = value.astype(jnp.bfloat16)
    return high, (value - high.astype(jnp.float32)).astype(jnp.bfloat16)


def select(a, b):
    parts = jnp.concatenate(two(a), axis=0)
    got = lax.dot_general(parts, b, NN, preferred_element_type=jnp.float32)
    return got[: a.shape[0]] + got[a.shape[0] :]


def constants():
    cell = np.arange(FACE)
    y, z = cell // FS, cell % FS
    t = np.arange(FS)
    faces = np.zeros((4 * FS, FACE), np.float32)
    for f, lanes in enumerate((t, FACE - FS + t, t * FS, t * FS + FS - 1)):
        faces[f * FS + t, lanes] = 1.0
    inside = np.zeros((FACE, FACE), np.float32)
    for dy, dz in ((1, 0), (-1, 0), (0, 1), (0, -1)):
        ok = (y + dy >= 0) & (y + dy < FS) & (z + dz >= 0) & (z + dz < FS)
        inside[cell[ok], (y + dy)[ok] * FS + (z + dz)[ok]] = 1.0
    coarse = y // 2 * HALF + z // 2
    upsample = np.zeros((HALF * HALF, FACE), np.float32)
    upsample[coarse, cell] = 1.0
    halves = np.zeros((128, 2 * FACE), np.float32)
    for m in range(4):
        c = np.arange(32)
        halves[32 * m + c, 64 * m + c] = 1.0
        halves[32 * m + c, FACE + 64 * m + 32 + c] = 1.0
    return faces, inside, upsample * 0.125, halves


FACES, INSIDE, AVERAGE, HALVES = constants()


def call(kernel, name, shapes, args, specs, scratch=(), out_specs=None, limit=24 << 20):
    return pl.pallas_call(
        kernel,
        out_shape=[
            jax.ShapeDtypeStruct(s[:-1], s[-1])
            if not isinstance(s[-1], int)
            else jax.ShapeDtypeStruct(s, jnp.float32)
            for s in shapes
        ],
        in_specs=specs,
        out_specs=out_specs or [VMEM] * len(shapes),
        scratch_shapes=list(scratch),
        compiler_params=pltpu.CompilerParams(vmem_limit_bytes=limit),
        name=name,
    )(*args)


def split(value):
    high = value.astype(jnp.bfloat16)
    rest = value - high.astype(jnp.float32)
    middle = rest.astype(jnp.bfloat16)
    low = (rest - middle.astype(jnp.float32)).astype(jnp.bfloat16)
    return high, middle, low


def gather_kernel(ids, patch, lists, out, hot):
    species = patch.shape[0]
    row = lax.broadcasted_iota(jnp.int32, (species, FACE), 0)
    lane = lax.broadcasted_iota(jnp.int32, (species, FACE), 1)
    place = ((lane == row) | (lane == row + 192)).astype(jnp.float32)
    turned = mm(patch[:, 0, :], place, TN)
    parts = jnp.concatenate(
        [jnp.concatenate(split(turned[:, 128 * h : 128 * h + 128]), axis=1) for h in range(2)],
        axis=0,
    )
    entries = lists[:, 0, :].astype(jnp.float32) - (ids[0] * FACE).astype(jnp.float32)
    across = entries[:, 0:128].T
    beside = entries[:, 128:160].T
    entries = jnp.concatenate(
        [
            jnp.maximum(across[0:64], across[64:128]),
            jnp.maximum(beside[0:8], beside[8:16]),
            jnp.maximum(beside[16:24], beside[24:32]),
        ],
        axis=0,
    )
    cell = lax.broadcasted_iota(jnp.int32, (SLOT, FACE), 1).astype(jnp.float32)
    groups = out.shape[0]
    for g in range(0, groups, 2):
        pair = [
            jnp.concatenate(
                [
                    (cell == entries[SLOT * h : SLOT * h + SLOT, k : k + 1]).astype(jnp.float32)
                    for h in range(2)
                ],
                axis=1,
            )
            for k in (g, g + 1)
        ]
        hot[SLOT * g : SLOT * g + 2 * SLOT, :] = jnp.concatenate(pair, axis=0).astype(jnp.bfloat16)
    step = 8
    for g in range(0, groups, step):
        got = jnp.dot(
            hot[SLOT * g : SLOT * (g + step), :], parts, preferred_element_type=jnp.float32
        )
        got = got[:, 0:128] + got[:, 128:256] + got[:, 256:384]
        for k in range(step):
            out[g + k] = got[SLOT * k : SLOT * k + SLOT]


def prepare_kernel(ids, owned, diffusion, stoich, orders, scale, stoich_out, orders_out, sources):
    me = ids[0]
    found = [jnp.int32(-1)] * 4
    for g in range(owned.shape[1]):
        entry = owned[0, g]
        found = [jnp.where(entry == me * 4 + m, g, found[m]) for m in range(4)]
    for m in range(4):
        sources[0, m] = found[m]
    d = diffusion[...]
    species = d.shape[0]
    column = jnp.concatenate([d, jnp.zeros((PAD - species, 1), jnp.float32)], axis=0)

    def total(value):
        return jnp.sum(jnp.sum(value, axis=0, keepdims=True), axis=1, keepdims=True)

    wide = 1.0 + 12.0 * jnp.max(column, axis=0, keepdims=True)
    s, o = stoich[...], orders[...]
    wide = wide + jnp.sqrt(total(s * s)) * jnp.sqrt(total(o * o))
    unit = 32.0 / wide
    reactions = s.shape[1]
    high, low = two(jnp.concatenate([s * unit, jnp.zeros((PAD - species, reactions))], axis=0))
    stoich_out[...] = jnp.concatenate([high, low], axis=0)
    o = jnp.concatenate([o, jnp.zeros((PAD - species, reactions))], axis=0).T
    high, low = two(o)
    orders_out[...] = jnp.concatenate([high, high, low], axis=1)
    lane = lax.broadcasted_iota(jnp.int32, (PAD, 128), 1)
    row = lax.broadcasted_iota(jnp.int32, (PAD, 1), 0)
    diagonal = jnp.where(row < species, unit * (1.0 + 6.0 * column), 0.0)
    value = jnp.where(lane == 0, diagonal, 0.0)
    value = jnp.where(lane == 1, unit * column, value)
    value = jnp.where(lane == 2, SHIFT * unit, value)
    value = jnp.where(lane == 3, column, value)
    value = jnp.where(lane == 4, unit, value)
    scale[0:PAD, :] = value
    scale[PAD:, :] = value


def mix(a, b, keep, shift):
    return jnp.where(keep, a, b) + pltpu.roll(jnp.where(keep, b, a), shift, 0)


def fetch(inverse, inv, arrived):
    count = inverse.shape[0]
    copies = []
    for block in range(PAD // 8):
        part = pl.ds(8 * block, min(8, count - 8 * block))
        copies.append(pltpu.make_async_copy(inverse.at[part], inv.at[part], arrived.at[block]))
    for copy in copies:
        copy.start()
    return copies


def apply_inverse(copies, inv, rows, u):
    count, depth = inv.shape[0], inv.shape[1]
    full = depth // 8
    row = lax.broadcasted_iota(jnp.int32, (8, 128), 0)
    bit2, bit1, bit0 = (row & 4) == 0, (row & 2) == 0, (row & 1) == 0
    zero = jnp.zeros((8, 128), jnp.float32)
    for block in range(PAD // 8):
        copies[block].wait()
        for half in range(2):
            lanes = slice(128 * half, 128 * half + 128)
            w = [rows[half, 8 * k : 8 * k + 8, :] for k in range(full + 1)]

            def one(i):
                if i >= count:
                    return zero
                m = inv[i, :, lanes].astype(jnp.float32)
                total = m[0:8] * w[0]
                for k in range(1, full):
                    total = total + m[8 * k : 8 * k + 8] * w[k]
                last = m[8 * full : depth]
                last = jnp.concatenate([last, zero[last.shape[0] :]], axis=0)
                return total + last * w[full]

            a = [one(8 * block + d) for d in range(8)]
            b = [mix(a[d], a[d + 2], bit1, 6) for d in (0, 1, 4, 5)]
            c = [mix(b[d], b[d + 2], bit2, 4) for d in range(2)]
            u[8 * block : 8 * block + 8, lanes] = jnp.where(bit0, c[0], pltpu.roll(c[1], 1, 0))
            u[PAD + 8 * block : PAD + 8 * block + 8, lanes] = jnp.where(
                bit0, pltpu.roll(c[0], 7, 0), c[1]
            )


def interleave(rows, field):
    for half in range(2):
        lanes = slice(128 * half, 128 * half + 128)
        rows.at[half][pl.ds(0, PAD, stride=2), :] = field[:PAD, lanes]
        rows.at[half][pl.ds(1, PAD, stride=2), :] = field[PAD:, lanes]


def separate(rows):
    planes = [
        jnp.concatenate([rows.at[h][pl.ds(x, PAD, stride=2), :] for h in range(2)], axis=1)
        for x in range(2)
    ]
    return jnp.concatenate(planes, axis=0)


def start(pairs, semaphores):
    copies = [
        pltpu.make_async_copy(source, target, semaphores.at[k])
        for k, (source, target) in enumerate(pairs)
    ]
    for copy in copies:
        copy.start()
    return copies


def precondition(meta, fetched, inv, image, faces, w_out, near, far, u_out, slots, w, u, planes, rows, sent):
    w[...] = image
    copies = [pltpu.make_async_copy(w, w_out, sent.at[0])]
    copies[0].start()
    interleave(rows, image)
    apply_inverse(fetched, inv, rows, u)
    even = meta[5, 1] % 2
    lower = pl.multiple_of(even * PAD, 8)
    upper = pl.multiple_of(PAD - even * PAD, 8)
    copies.append(pltpu.make_async_copy(u.at[pl.ds(upper, PAD)], near, sent.at[1]))
    copies.append(pltpu.make_async_copy(u.at[pl.ds(lower, PAD)], far, sent.at[2]))
    copies.append(pltpu.make_async_copy(u, u_out, sent.at[3]))
    for copy in copies[1:]:
        copy.start()
    face = faces[...].astype(jnp.bfloat16)
    planes[:, 0:ROWS] = lax.dot_general(
        jnp.concatenate([face, face], axis=1),
        jnp.concatenate(two(u[...]), axis=1),
        NT,
        preferred_element_type=jnp.float32,
    )
    for f in range(4):
        other = meta[f, meta[5, 0]]

        @pl.when(other >= 0)
        def _():
            pltpu.make_async_copy(
                planes.at[pl.ds(FS * f, FS)], slots.at[jnp.maximum(other, 0)], sent.at[4 + f]
            ).start()

    for f in range(4):
        other = meta[f, meta[5, 0]]

        @pl.when(other >= 0)
        def _():
            pltpu.make_async_copy(
                planes.at[pl.ds(FS * f, FS)], slots.at[jnp.maximum(other, 0)], sent.at[4 + f]
            ).wait()

    for copy in copies:
        copy.wait()


def first_kernel(*refs):
    outside, inverse, outs, inside = refs[:5], refs[5], refs[6:11], refs[11:16]
    arrived, inv, blocks, w, u, planes, rows, sent = refs[16:]
    copies = start(zip(outside, inside), arrived)
    fetched = fetch(inverse, inv, blocks)
    for copy in copies:
        copy.wait()
    meta, received, source, scale, faces = inside
    values = received[0]
    for g in range(1, received.shape[0]):
        values = values + received[g]
    me = meta[5, 0]
    row = lax.broadcasted_iota(jnp.int32, (SLOT, FACE), 0)
    cell = lax.broadcasted_iota(jnp.int32, (SLOT, FACE), 1)
    y, z = cell // FS, cell % FS
    coarse = y // 2 * HALF + z // 2
    first = 64 - SLOT
    y_face = jnp.where(meta[0, me] < 0, 0, FS - 1)
    z_face = jnp.where(meta[2, me] < 0, 0, FS - 1)
    sides = ((y == y_face) & (row == first + z // 2)).astype(jnp.float32)
    sides = sides + ((z == z_face) & (row == first + HALF + y // 2)).astype(jnp.float32)
    ends = [coarse == row, (coarse == row + SLOT) & (row < first)]
    ends = [end.astype(jnp.float32) for end in ends]
    across = mm(values, jnp.concatenate([ends[0], ends[1], sides], axis=1), TN)
    beside = across[64 : 64 + PAD, 2 * FACE :]
    across = across[0:PAD, :FACE] + across[64 : 64 + PAD, FACE : 2 * FACE]
    bottom = jnp.where(meta[5, 1] == 0, 1.0, 0.0)
    boundary = jnp.concatenate([beside + bottom * across, beside + (1.0 - bottom) * across], axis=0)
    species = source.shape[0]
    for half in range(2):
        rows[half, 0:species, :] = source[:, 128 * half : 128 * half + 128]
        rows[half, species:ROWS, :] = jnp.zeros((ROWS - species, 128), jnp.float32)
    right = separate(rows) + scale[:, 3:4] * boundary
    precondition(meta, fetched, inv, right, faces, *outs, w, u, planes, rows, sent)


def dots(vectors, last):
    lane = lax.broadcasted_iota(jnp.int32, (8, 128), 1)
    line = jnp.zeros((8, 128), jnp.float32)
    count = len(vectors)
    for b, vector in enumerate(vectors + [last]):
        product = last * vector
        total = product[0:8]
        for k in range(8, ROWS, 8):
            total = total + product[k : k + 8]
        total = jnp.sum(total[:, :128] + total[:, 128:], axis=0, keepdims=True)
        total = jnp.sum(total, axis=1, keepdims=True)
        line = jnp.where(lane == count * (count + 1) // 2 + b, total, line)
    return line


def local_kernel(j, *refs):
    count = 7 + j
    outside, (part, line), inside_refs = refs[:count], refs[count : count + 2], refs[count + 2 :]
    result, summed, arrived, sent = inside_refs[count:]
    copies = start(zip(outside, inside_refs[:count]), arrived)
    u, w, scale, inside, orders, stoich, rates = inside_refs[:7]
    for copy in copies:
        copy.wait()
    field = u[...]
    lower, upper = field[:PAD], field[PAD:]
    total = select(field, inside[...].astype(jnp.bfloat16))
    total = total + jnp.concatenate([field[PAD:], field[:PAD]], axis=0)
    both = jnp.concatenate([lower, upper], axis=1)
    high, low = two(both)
    progress = jnp.dot(
        orders[...], jnp.concatenate([high, low, high], axis=0), preferred_element_type=jnp.float32
    )
    high, low = two(progress * rates[...])
    chemistry = jnp.dot(stoich[...], high, preferred_element_type=jnp.float32)
    chemistry = chemistry[:PAD] + chemistry[PAD:]
    chemistry = chemistry + jnp.dot(stoich[:PAD, :], low, preferred_element_type=jnp.float32)
    chemistry = jnp.concatenate([chemistry[:, :FACE], chemistry[:, FACE:]], axis=0)
    result[...] = (
        scale[:, 0:1] * field - scale[:, 1:2] * total - chemistry - scale[:, 2:3] * w[...]
    )
    copies = start([(result, part)], sent)
    summed[...] = dots([ref[...] for ref in inside_refs[7:count]], w[...])
    copy = pltpu.make_async_copy(summed, line, sent.at[1])
    copy.start()
    copy.wait()
    copies[0].wait()


def image_of(outside, inside, arrived, blocks=None):
    meta, received, ends, part, scale, faces = inside
    targets = (meta, received, ends.at[0], ends.at[1], part, scale, faces)
    copies = start(zip(outside, targets), arrived)
    fetched = fetch(*blocks) if blocks else None
    for copy in copies:
        copy.wait()
    me, box = meta[5, 0], meta[5, 1]
    ghosts = []
    for f in range(4):
        other = meta[f, me]
        plane = received[jnp.maximum(other, 0), :, 0:ROWS]
        ghosts.append(jnp.where(jnp.full((FS, ROWS), other, jnp.int32) >= 0, plane, 0.0))
    face = faces[...].astype(jnp.bfloat16)
    total = lax.dot_general(
        jnp.concatenate(two(jnp.concatenate(ghosts, axis=0)), axis=0),
        jnp.concatenate([face, face], axis=0),
        TN,
        preferred_element_type=jnp.float32,
    )
    even = 1 - box % 2
    low = jnp.where(box == 0, 0.0, 1.0) * ends[even]
    high = jnp.where(box == meta[5, 2], 0.0, 1.0) * ends[1 - even]
    total = total + jnp.concatenate([low, high], axis=0)
    return part[...] - scale[:, 1:2] * total, fetched


def combine_kernel(*refs):
    outside, inverse, outs, inside = refs[:7], refs[7], refs[8:13], refs[13:19]
    arrived, inv, blocks, w, u, planes, rows, sent = refs[19:]
    image, fetched = image_of(outside, inside, arrived, (inverse, inv, blocks))
    precondition(inside[0], fetched, inv, image, inside[5], *outs, w, u, planes, rows, sent)


def last_kernel(*refs):
    outside, basis, lines, out, inside = refs[:7], refs[7:11], refs[11:15], refs[15], refs[16:22]
    arrived, held, sums, landed = refs[22:]
    pairs = [(basis[k], held.at[k]) for k in range(ITERS)]
    pairs += [(lines[k], sums.at[k]) for k in range(ITERS)]
    copies = start(pairs, landed)
    image, _ = image_of(outside, inside, arrived)
    for copy in copies:
        copy.wait()
    line = dots([held[k] for k in range(ITERS)], image)
    for k in range(ITERS):
        line = line + sums[k]
    out[...] = jnp.broadcast_to(line[0:1], out.shape)


def solve(gram, shift):
    def g(a, b):
        return gram[(max(a, b), min(a, b))]

    n = ITERS
    target = [g(a + 1, 0) + shift * g(a, 0) for a in range(n)]
    normal = {}
    for a in range(n):
        for b in range(a + 1):
            normal[a, b] = (
                g(a + 1, b + 1) + shift * (g(a + 1, b) + g(a, b + 1)) + shift * shift * g(a, b)
            )
    size = [lax.rsqrt(normal[a, a]) for a in range(n)]
    target = [target[a] * size[a] for a in range(n)]
    lower = {}
    inverse = [None] * n
    for a in range(n):
        for b in range(a + 1):
            value = normal[a, b] * size[a] * size[b]
            for c in range(b):
                value = value - lower[a, c] * lower[b, c]
            if a == b:
                inverse[a] = lax.rsqrt(value)
            else:
                lower[a, b] = value * inverse[b]
    half = []
    for a in range(n):
        value = target[a]
        for c in range(a):
            value = value - lower[a, c] * half[c]
        half.append(value * inverse[a])
    result = [None] * n
    for a in reversed(range(n)):
        value = half[a]
        for c in range(a + 1, n):
            value = value - lower[c, a] * result[c]
        result[a] = value * inverse[a]
    return [result[a] * size[a] for a in range(n)]


def finish_kernel(*refs):
    n = ITERS
    outside, outs, inside = refs[: n + 4], refs[n + 4 : n + 6], refs[n + 6 : n + 11]
    arrived, result, mean, rows, sent = refs[n + 11 :]
    lines, scale, meta, average, fields = inside
    copies = start(
        zip(outside, [lines, scale, meta, average] + [fields.at[k] for k in range(n)]), arrived
    )
    copies[0].wait()
    line = jnp.sum(lines[...], axis=0, keepdims=True)
    gram = {}
    k = 0
    for a in range(ITERS + 1):
        for b in range(a + 1):
            gram[a, b] = line[:, k : k + 1]
            k += 1
    copies[1].wait()
    weights = solve(gram, scale[0:1, 2:3])
    factor = scale[0:1, 4:5]
    for copy in copies[2:]:
        copy.wait()
    total = (weights[0] * factor) * fields[0]
    for k in range(1, ITERS):
        total = total + (weights[k] * factor) * fields[k]
    summed = total[:PAD] + total[PAD:]
    blank = jnp.zeros((64 - PAD, FACE), jnp.float32)
    spread = jnp.concatenate([summed, blank, summed, blank], axis=0)
    weight = average[...].astype(jnp.bfloat16)
    got = lax.dot_general(
        jnp.concatenate([weight, weight], axis=1),
        jnp.concatenate(two(spread), axis=1),
        NT,
        preferred_element_type=jnp.float32,
    )
    lane = lax.broadcasted_iota(jnp.int32, (32, 128), 1)
    mean[...] = jnp.where(lane < 64, got[:32], got[32:])
    home = meta[4, meta[5, 0]] // 4
    copies = start([(mean, outs[1].at[home])], sent)
    interleave(rows, total)
    for half in range(2):
        lanes = slice(128 * half, 128 * half + 128)
        result[:, lanes] = rows[half, 0 : result.shape[0], :]
    copies.append(pltpu.make_async_copy(result, outs[0], sent.at[1]))
    copies[1].start()
    for copy in copies:
        copy.wait()


def update_kernel(*refs):
    outside, out, inside, arrived = refs[:4], refs[4], refs[5:9], refs[9]
    copies = start(zip(outside, inside), arrived)
    for copy in copies:
        copy.wait()
    sources, received, patch, halves = inside
    lane = lax.broadcasted_iota(jnp.int32, (1, FACE), 1)
    covered = jnp.zeros((1, FACE), jnp.int32)
    blocks = []
    for m in range(4):
        source = sources[0, m]
        block = received[jnp.maximum(source, 0)]
        blocks.append(jnp.where(jnp.full((32, 128), source, jnp.int32) >= 0, block, 0.0))
        covered = jnp.where(lane // 64 == m, source, covered)
    stacked = jnp.concatenate(blocks, axis=0)
    species = patch.shape[0]
    half = halves[...].astype(jnp.bfloat16)
    got = lax.dot_general(
        jnp.concatenate(two(stacked), axis=0),
        jnp.concatenate([half, half], axis=0),
        TN,
        preferred_element_type=jnp.float32,
    )
    got = got[0:species, :FACE] + got[64 : 64 + species, FACE:]
    out[:, 0, :] = jnp.where(covered >= 0, got, patch[...])


def on_device(
    source_term,
    diffusion,
    stoich,
    orders,
    rates,
    precond,
    coarse_field,
    neighbours,
    ghost_list,
    average_list,
):
    species, reactions = stoich.shape
    groups = lax.axis_size("grp")
    boxes = lax.axis_size("box")
    me = lax.axis_index("grp")
    box = lax.axis_index("box")
    f32 = jnp.float32

    ids = jnp.stack([me, box, jnp.asarray(boxes - 1, box.dtype)]).astype(jnp.int32)
    links = neighbours.T
    owned = average_list.T
    even_swap = [(i, i ^ 1) for i in range(boxes)]
    odd_swap = [(i, (i + (1 if i % 2 else -1)) % boxes) for i in range(boxes)]

    meta = jnp.concatenate([links, owned, jnp.pad(ids, (0, groups - 3))[None]], axis=0)
    meta = jnp.pad(meta, ((0, 2), (0, 128 - groups)))

    def exchange(slots):
        return lax.all_to_all(slots, "grp", 0, 0, tiled=True)

    (asked,) = call(
        gather_kernel, "gather", [(groups, SLOT, 128)], (ids, coarse_field, ghost_list), [SMEM] + [VMEM] * 2,
        [pltpu.VMEM((groups * SLOT, 2 * FACE), jnp.bfloat16)],
    )
    received = exchange(asked)
    scale, stoich_s, orders_s, sources = call(
        prepare_kernel,
        "prepare",
        [(ROWS, 128), (2 * PAD, reactions, jnp.bfloat16), (reactions, 3 * PAD, jnp.bfloat16), (8, 128, jnp.int32)],
        (ids, owned, diffusion.reshape(species, 1), stoich, orders.T),
        [SMEM] * 2 + [VMEM] * 3,
        (),
        [VMEM] * 3 + [SMEM],
    )
    rates_s = rates.reshape(reactions, 2 * FACE)
    inverse = precond.reshape(species, 2 * species, FACE)
    source = source_term.reshape(2 * species, FACE)
    faces = jnp.asarray(FACES)
    inside = jnp.asarray(INSIDE)
    outs = [(ROWS, FACE), (PAD, FACE), (PAD, FACE), (ROWS, FACE), (groups, FS, 128)]
    cells = pltpu.VMEM((ROWS, FACE), f32)
    rows = [pltpu.VMEM((2, ROWS, 128), f32)]
    held = [pltpu.VMEM(inverse.shape, inverse.dtype), pltpu.SemaphoreType.DMA((PAD // 8,))]
    work = [cells, cells, pltpu.VMEM((4 * FS, 128), f32)] + rows + [pltpu.SemaphoreType.DMA((8,))]
    landing = [
        pltpu.SMEM(meta.shape, jnp.int32),
        pltpu.VMEM((groups, FS, 128), f32),
        pltpu.VMEM((2, PAD, FACE), f32),
        cells,
        pltpu.VMEM((ROWS, 128), f32),
        pltpu.VMEM((4 * FS, FACE), f32),
        pltpu.SemaphoreType.DMA((7,)),
    ]
    w, near, far, u, slots = call(
        first_kernel,
        "first",
        outs,
        (meta, received, source, scale, faces, inverse),
        [HBM] * 6,
        [pltpu.SMEM(meta.shape, jnp.int32)]
        + [pltpu.VMEM(x.shape, f32) for x in (received, source, scale, faces)]
        + [pltpu.SemaphoreType.DMA((5,))]
        + held
        + work,
        [HBM] * 5,
        WHOLE,
    )
    basis, directions, lines = [w], [u], []
    for j in range(ITERS):
        received = exchange(slots)
        near_in = lax.ppermute(near, "box", even_swap)
        far_in = lax.ppermute(far, "box", odd_swap)
        operands = (u, w, scale, inside, orders_s, stoich_s, rates_s) + tuple(basis[:-1])
        count = len(operands)
        part, line = call(
            functools.partial(local_kernel, j),
            "local%d" % j,
            [(ROWS, FACE), (8, 128)],
            operands,
            [HBM] * count,
            [pltpu.VMEM(x.shape, x.dtype) for x in operands]
            + [cells, pltpu.VMEM((8, 128), f32)]
            + [pltpu.SemaphoreType.DMA((count,)), pltpu.SemaphoreType.DMA((2,))],
            [HBM] * 2,
            WHOLE,
        )
        lines.append(line)
        shared = (meta, received, near_in, far_in, part, scale, faces)
        if j + 1 < ITERS:
            w, near, far, u, slots = call(
                combine_kernel,
                "combine%d" % j,
                outs,
                shared + (inverse,),
                [HBM] * 8,
                landing + held + work,
                [HBM] * 5,
                WHOLE,
            )
            basis.append(w)
            directions.append(u)
        else:
            (lines,) = call(
                last_kernel,
                "last",
                [(groups * boxes, 128)],
                shared + tuple(basis) + tuple(lines),
                [HBM] * 15,
                landing
                + [pltpu.VMEM((ITERS, ROWS, FACE), f32), pltpu.VMEM((ITERS, 8, 128), f32)]
                + [pltpu.SemaphoreType.DMA((2 * ITERS,))],
                limit=WHOLE,
            )
    lines = lax.all_to_all(lines, ("grp", "box"), 0, 0, tiled=True)
    average = jnp.asarray(AVERAGE)
    correction, slots = call(
        finish_kernel,
        "finish",
        [(2 * species, FACE), (groups, 32, 128)],
        (lines, scale, meta, average) + tuple(directions),
        [HBM] * (4 + ITERS),
        [pltpu.VMEM(lines.shape, f32), pltpu.VMEM((ROWS, 128), f32)]
        + [pltpu.SMEM(meta.shape, jnp.int32), pltpu.VMEM(average.shape, f32)]
        + [pltpu.VMEM((ITERS, ROWS, FACE), f32), pltpu.SemaphoreType.DMA((ITERS + 4,))]
        + [pltpu.VMEM((2 * species, FACE), f32), pltpu.VMEM((32, 128), f32)]
        + rows
        + [pltpu.SemaphoreType.DMA((2,))],
        [HBM] * 2,
        WHOLE,
    )
    received = exchange(slots)
    halves = jnp.asarray(HALVES)
    (updated,) = call(
        update_kernel,
        "update",
        [(species, 1, FACE)],
        (sources, received, coarse_field.reshape(species, FACE), halves),
        [HBM] * 4,
        [pltpu.SMEM((8, 128), jnp.int32), pltpu.VMEM(received.shape, f32)]
        + [pltpu.VMEM((species, FACE), f32), pltpu.VMEM(halves.shape, f32)]
        + [pltpu.SemaphoreType.DMA((4,))],
        limit=WHOLE,
    )
    return correction.reshape(species, 1, 2, FACE), updated


def solution(mesh):
    placed = (
        P(None, "grp", "box", None),
        P(),
        P(),
        P(),
        P(None, "grp", "box", None),
        P(None, None, "grp", "box", None),
        P(None, "grp", "box"),
        P(),
        P(None, "box", None),
        P(None, "box"),
    )
    return jax.shard_map(
        on_device,
        mesh=mesh,
        in_specs=placed,
        out_specs=(P(None, "grp", "box", None), P(None, "grp", "box")),
        check_vma=False,
    )
```

```python
import functools

import jax
import jax.numpy as jnp
import numpy as np
from jax import lax
from jax.experimental import pallas as pl
from jax.experimental.pallas import tpu as pltpu
from jax.sharding import PartitionSpec as P

FS = 16
ITERS = 4
SHIFT = 1.0
HALF = FS // 2
FACE = FS * FS
PAD = 56
ROWS = 2 * PAD
SLOT = 40
WHOLE = 66900000
EXACT = lax.Precision.HIGHEST
HBM = pl.BlockSpec(memory_space=pltpu.HBM)
VMEM = pl.BlockSpec(memory_space=pltpu.VMEM)
SMEM = pl.BlockSpec(memory_space=pltpu.SMEM)

NN = (((1,), (0,)), ((), ()))
NT = (((1,), (1,)), ((), ()))
TN = (((0,), (0,)), ((), ()))


def mm(a, b, dims=NN):
    return lax.dot_general(a, b, dims, precision=EXACT, preferred_element_type=jnp.float32)


def two(value):
    high = value.astype(jnp.bfloat16)
    return high, (value - high.astype(jnp.float32)).astype(jnp.bfloat16)


def select(a, b):
    parts = jnp.concatenate(two(a), axis=0)
    got = lax.dot_general(parts, b, NN, preferred_element_type=jnp.float32)
    return got[: a.shape[0]] + got[a.shape[0] :]


def constants():
    cell = np.arange(FACE)
    y, z = cell // FS, cell % FS
    t = np.arange(FS)
    faces = np.zeros((4 * FS, FACE), np.float32)
    for f, lanes in enumerate((t, FACE - FS + t, t * FS, t * FS + FS - 1)):
        faces[f * FS + t, lanes] = 1.0
    inside = np.zeros((FACE, FACE), np.float32)
    for dy, dz in ((1, 0), (-1, 0), (0, 1), (0, -1)):
        ok = (y + dy >= 0) & (y + dy < FS) & (z + dz >= 0) & (z + dz < FS)
        inside[cell[ok], (y + dy)[ok] * FS + (z + dz)[ok]] = 1.0
    coarse = y // 2 * HALF + z // 2
    upsample = np.zeros((HALF * HALF, FACE), np.float32)
    upsample[coarse, cell] = 1.0
    halves = np.zeros((128, 2 * FACE), np.float32)
    for m in range(4):
        c = np.arange(32)
        halves[32 * m + c, 64 * m + c] = 1.0
        halves[32 * m + c, FACE + 64 * m + 32 + c] = 1.0
    return faces, inside, upsample * 0.125, halves


FACES, INSIDE, AVERAGE, HALVES = constants()


def call(kernel, name, shapes, args, specs, scratch=(), out_specs=None, limit=24 << 20):
    return pl.pallas_call(
        kernel,
        out_shape=[
            jax.ShapeDtypeStruct(s[:-1], s[-1])
            if not isinstance(s[-1], int)
            else jax.ShapeDtypeStruct(s, jnp.float32)
            for s in shapes
        ],
        in_specs=specs,
        out_specs=out_specs or [VMEM] * len(shapes),
        scratch_shapes=list(scratch),
        compiler_params=pltpu.CompilerParams(vmem_limit_bytes=limit),
        name=name,
    )(*args)


def split(value):
    high = value.astype(jnp.bfloat16)
    rest = value - high.astype(jnp.float32)
    middle = rest.astype(jnp.bfloat16)
    low = (rest - middle.astype(jnp.float32)).astype(jnp.bfloat16)
    return high, middle, low


def gather_kernel(ids, patch_out, lists_out, out, patch, lists, arrived, hot, slots, sent):
    copies = start([(patch_out, patch), (lists_out, lists)], arrived)
    for copy in copies:
        copy.wait()
    species = patch.shape[0]
    row = lax.broadcasted_iota(jnp.int32, (species, FACE), 0)
    lane = lax.broadcasted_iota(jnp.int32, (species, FACE), 1)
    place = ((lane == row) | (lane == row + 192)).astype(jnp.float32)
    turned = mm(patch[:, 0, :], place, TN)
    parts = jnp.concatenate(
        [jnp.concatenate(split(turned[:, 128 * h : 128 * h + 128]), axis=1) for h in range(2)],
        axis=0,
    )
    entries = lists[:, 0, :].astype(jnp.float32) - (ids[0] * FACE).astype(jnp.float32)
    across = entries[:, 0:128].T
    beside = entries[:, 128:160].T
    entries = jnp.concatenate(
        [
            jnp.maximum(across[0:64], across[64:128]),
            jnp.maximum(beside[0:8], beside[8:16]),
            jnp.maximum(beside[16:24], beside[24:32]),
        ],
        axis=0,
    )
    cell = lax.broadcasted_iota(jnp.int32, (SLOT, FACE), 1).astype(jnp.float32)
    groups = out.shape[0]
    for g in range(0, groups, 2):
        pair = [
            jnp.concatenate(
                [
                    (cell == entries[SLOT * h : SLOT * h + SLOT, k : k + 1]).astype(jnp.float32)
                    for h in range(2)
                ],
                axis=1,
            )
            for k in (g, g + 1)
        ]
        hot[SLOT * g : SLOT * g + 2 * SLOT, :] = jnp.concatenate(pair, axis=0).astype(jnp.bfloat16)
    step = 8
    copies = []
    for g in range(0, groups, step):
        got = jnp.dot(
            hot[SLOT * g : SLOT * (g + step), :], parts, preferred_element_type=jnp.float32
        )
        got = got[:, 0:128] + got[:, 128:256] + got[:, 256:384]
        for k in range(step):
            slots[g + k] = got[SLOT * k : SLOT * k + SLOT]
        part = pl.ds(g, step)
        copies.append(pltpu.make_async_copy(slots.at[part], out.at[part], sent.at[g // step]))
        copies[-1].start()
    for copy in copies:
        copy.wait()


def prepare_kernel(ids, owned, diffusion, stoich, orders, scale, stoich_out, orders_out, sources):
    me = ids[0]
    group = lax.broadcasted_iota(jnp.int32, owned.shape, 1)
    for m in range(4):
        sources[0, m] = jnp.max(jnp.where(owned[...] == me * 4 + m, group, -1))
    d = diffusion[...]
    species = d.shape[1]
    row = lax.broadcasted_iota(jnp.int32, (PAD, species), 0)
    lane = lax.broadcasted_iota(jnp.int32, (PAD, species), 1)
    column = jnp.sum(jnp.where(row == lane, d, 0.0), axis=1, keepdims=True)

    def total(value):
        return jnp.sum(jnp.sum(value, axis=0, keepdims=True), axis=1, keepdims=True)

    wide = 1.0 + 12.0 * jnp.max(column, axis=0, keepdims=True)
    s, o = stoich[...], orders[...]
    wide = wide + jnp.sqrt(total(s * s)) * jnp.sqrt(total(o * o))
    unit = 32.0 / wide
    reactions = s.shape[1]
    high, low = two(jnp.concatenate([s * unit, jnp.zeros((PAD - species, reactions))], axis=0))
    stoich_out[...] = jnp.concatenate([high, low], axis=0)
    o = jnp.concatenate([o, jnp.zeros((PAD - species, reactions))], axis=0).T
    high, low = two(o)
    orders_out[...] = jnp.concatenate([high, high, low], axis=1)
    lane = lax.broadcasted_iota(jnp.int32, (PAD, 128), 1)
    row = lax.broadcasted_iota(jnp.int32, (PAD, 1), 0)
    diagonal = jnp.where(row < species, unit * (1.0 + 6.0 * column), 0.0)
    value = jnp.where(lane == 0, diagonal, 0.0)
    value = jnp.where(lane == 1, unit * column, value)
    value = jnp.where(lane == 2, SHIFT * unit, value)
    value = jnp.where(lane == 3, column, value)
    value = jnp.where(lane == 4, unit, value)
    scale[0:PAD, :] = value
    scale[PAD:, :] = value


def mix(a, b, keep, shift):
    return jnp.where(keep, a, b) + pltpu.roll(jnp.where(keep, b, a), shift, 0)


def fetch(inverse, inv, arrived):
    count = inverse.shape[0]
    copies = []
    for block in range(PAD // 8):
        part = pl.ds(8 * block, min(8, count - 8 * block))
        copies.append(pltpu.make_async_copy(inverse.at[part], inv.at[part], arrived.at[block]))
    for copy in copies:
        copy.start()
    return copies


def apply_inverse(copies, inv, rows, u):
    count, depth = inv.shape[0], inv.shape[1]
    full = depth // 8
    row = lax.broadcasted_iota(jnp.int32, (8, 128), 0)
    bit2, bit1, bit0 = (row & 4) == 0, (row & 2) == 0, (row & 1) == 0
    zero = jnp.zeros((8, 128), jnp.float32)
    for block in range(PAD // 8):
        copies[block].wait()
        for half in range(2):
            lanes = slice(128 * half, 128 * half + 128)
            w = [rows[half, 8 * k : 8 * k + 8, :] for k in range(full + 1)]

            def one(i):
                if i >= count:
                    return zero
                m = inv[i, :, lanes].astype(jnp.float32)
                total = m[0:8] * w[0]
                for k in range(1, full):
                    total = total + m[8 * k : 8 * k + 8] * w[k]
                last = m[8 * full : depth]
                last = jnp.concatenate([last, zero[last.shape[0] :]], axis=0)
                return total + last * w[full]

            a = [one(8 * block + d) for d in range(8)]
            b = [mix(a[d], a[d + 2], bit1, 6) for d in (0, 1, 4, 5)]
            c = [mix(b[d], b[d + 2], bit2, 4) for d in range(2)]
            u[8 * block : 8 * block + 8, lanes] = jnp.where(bit0, c[0], pltpu.roll(c[1], 1, 0))
            u[PAD + 8 * block : PAD + 8 * block + 8, lanes] = jnp.where(
                bit0, pltpu.roll(c[0], 7, 0), c[1]
            )


def interleave(rows, field):
    for half in range(2):
        lanes = slice(128 * half, 128 * half + 128)
        rows.at[half][pl.ds(0, PAD, stride=2), :] = field[:PAD, lanes]
        rows.at[half][pl.ds(1, PAD, stride=2), :] = field[PAD:, lanes]


def separate(rows):
    planes = [
        jnp.concatenate([rows.at[h][pl.ds(x, PAD, stride=2), :] for h in range(2)], axis=1)
        for x in range(2)
    ]
    return jnp.concatenate(planes, axis=0)


def start(pairs, semaphores):
    copies = [
        pltpu.make_async_copy(source, target, semaphores.at[k])
        for k, (source, target) in enumerate(pairs)
    ]
    for copy in copies:
        copy.start()
    return copies


def precondition(meta, fetched, inv, image, faces, w_out, near, far, u_out, slots, w, u, planes, rows, sent):
    w[...] = image
    copies = [pltpu.make_async_copy(w, w_out, sent.at[0])]
    copies[0].start()
    interleave(rows, image)
    apply_inverse(fetched, inv, rows, u)
    even = meta[5, 1] % 2
    lower = pl.multiple_of(even * PAD, 8)
    upper = pl.multiple_of(PAD - even * PAD, 8)
    copies.append(pltpu.make_async_copy(u.at[pl.ds(upper, PAD)], near, sent.at[1]))
    copies.append(pltpu.make_async_copy(u.at[pl.ds(lower, PAD)], far, sent.at[2]))
    copies.append(pltpu.make_async_copy(u, u_out, sent.at[3]))
    for copy in copies[1:]:
        copy.start()
    face = faces[...].astype(jnp.bfloat16)
    planes[:, 0:ROWS] = lax.dot_general(
        jnp.concatenate([face, face], axis=1),
        jnp.concatenate(two(u[...]), axis=1),
        NT,
        preferred_element_type=jnp.float32,
    )
    for f in range(4):
        other = meta[f, meta[5, 0]]

        @pl.when(other >= 0)
        def _():
            pltpu.make_async_copy(
                planes.at[pl.ds(FS * f, FS)], slots.at[jnp.maximum(other, 0)], sent.at[4 + f]
            ).start()

    for f in range(4):
        other = meta[f, meta[5, 0]]

        @pl.when(other >= 0)
        def _():
            pltpu.make_async_copy(
                planes.at[pl.ds(FS * f, FS)], slots.at[jnp.maximum(other, 0)], sent.at[4 + f]
            ).wait()

    for copy in copies:
        copy.wait()


def first_kernel(*refs):
    outside, inverse, outs, inside = refs[:5], refs[5], refs[6:11], refs[11:16]
    arrived, inv, blocks, w, u, planes, rows, sent = refs[16:]
    copies = start(zip(outside, inside), arrived)
    fetched = fetch(inverse, inv, blocks)
    for copy in copies:
        copy.wait()
    meta, received, source, scale, faces = inside
    values = received[0]
    for g in range(1, received.shape[0]):
        values = values + received[g]
    me = meta[5, 0]
    row = lax.broadcasted_iota(jnp.int32, (SLOT, FACE), 0)
    cell = lax.broadcasted_iota(jnp.int32, (SLOT, FACE), 1)
    y, z = cell // FS, cell % FS
    coarse = y // 2 * HALF + z // 2
    first = 64 - SLOT
    y_face = jnp.where(meta[0, me] < 0, 0, FS - 1)
    z_face = jnp.where(meta[2, me] < 0, 0, FS - 1)
    sides = ((y == y_face) & (row == first + z // 2)).astype(jnp.float32)
    sides = sides + ((z == z_face) & (row == first + HALF + y // 2)).astype(jnp.float32)
    ends = [coarse == row, (coarse == row + SLOT) & (row < first)]
    ends = [end.astype(jnp.float32) for end in ends]
    across = mm(values, jnp.concatenate([ends[0], ends[1], sides], axis=1), TN)
    beside = across[64 : 64 + PAD, 2 * FACE :]
    across = across[0:PAD, :FACE] + across[64 : 64 + PAD, FACE : 2 * FACE]
    bottom = jnp.where(meta[5, 1] == 0, 1.0, 0.0)
    boundary = jnp.concatenate([beside + bottom * across, beside + (1.0 - bottom) * across], axis=0)
    species = source.shape[0]
    for half in range(2):
        rows[half, 0:species, :] = source[:, 128 * half : 128 * half + 128]
        rows[half, species:ROWS, :] = jnp.zeros((ROWS - species, 128), jnp.float32)
    right = separate(rows) + scale[:, 3:4] * boundary
    precondition(meta, fetched, inv, right, faces, *outs, w, u, planes, rows, sent)


def dots(vectors, last):
    lane = lax.broadcasted_iota(jnp.int32, (8, 128), 1)
    line = jnp.zeros((8, 128), jnp.float32)
    count = len(vectors)
    for b, vector in enumerate(vectors + [last]):
        product = last * vector
        total = product[0:8]
        for k in range(8, ROWS, 8):
            total = total + product[k : k + 8]
        total = jnp.sum(total[:, :128] + total[:, 128:], axis=0, keepdims=True)
        total = jnp.sum(total, axis=1, keepdims=True)
        line = jnp.where(lane == count * (count + 1) // 2 + b, total, line)
    return line


def local_kernel(j, *refs):
    count = 7 + j
    outside, (part, line), inside_refs = refs[:count], refs[count : count + 2], refs[count + 2 :]
    result, summed, arrived, sent = inside_refs[count:]
    copies = start(zip(outside, inside_refs[:count]), arrived)
    u, w, scale, inside, orders, stoich, rates = inside_refs[:7]
    for copy in copies:
        copy.wait()
    field = u[...]
    lower, upper = field[:PAD], field[PAD:]
    total = select(field, inside[...].astype(jnp.bfloat16))
    total = total + jnp.concatenate([field[PAD:], field[:PAD]], axis=0)
    both = jnp.concatenate([lower, upper], axis=1)
    high, low = two(both)
    progress = jnp.dot(
        orders[...], jnp.concatenate([high, low, high], axis=0), preferred_element_type=jnp.float32
    )
    progress = [progress[:, FACE * x : FACE * x + FACE] * rates[x] for x in range(2)]
    high, low = two(jnp.concatenate(progress, axis=1))
    chemistry = jnp.dot(stoich[...], high, preferred_element_type=jnp.float32)
    chemistry = chemistry[:PAD] + chemistry[PAD:]
    chemistry = chemistry + jnp.dot(stoich[:PAD, :], low, preferred_element_type=jnp.float32)
    chemistry = jnp.concatenate([chemistry[:, :FACE], chemistry[:, FACE:]], axis=0)
    result[...] = (
        scale[:, 0:1] * field - scale[:, 1:2] * total - chemistry - scale[:, 2:3] * w[...]
    )
    copies = start([(result, part)], sent)
    summed[...] = dots([ref[...] for ref in inside_refs[7:count]], w[...])
    copy = pltpu.make_async_copy(summed, line, sent.at[1])
    copy.start()
    copy.wait()
    copies[0].wait()


def image_of(outside, inside, arrived, blocks=None):
    meta, received, ends, part, scale, faces = inside
    targets = (meta, received, ends.at[0], ends.at[1], part, scale, faces)
    copies = start(zip(outside, targets), arrived)
    fetched = fetch(*blocks) if blocks else None
    for copy in copies:
        copy.wait()
    me, box = meta[5, 0], meta[5, 1]
    ghosts = []
    for f in range(4):
        other = meta[f, me]
        plane = received[jnp.maximum(other, 0), :, 0:ROWS]
        ghosts.append(jnp.where(jnp.full((FS, ROWS), other, jnp.int32) >= 0, plane, 0.0))
    face = faces[...].astype(jnp.bfloat16)
    total = lax.dot_general(
        jnp.concatenate(two(jnp.concatenate(ghosts, axis=0)), axis=0),
        jnp.concatenate([face, face], axis=0),
        TN,
        preferred_element_type=jnp.float32,
    )
    even = 1 - box % 2
    low = jnp.where(box == 0, 0.0, 1.0) * ends[even]
    high = jnp.where(box == meta[5, 2], 0.0, 1.0) * ends[1 - even]
    total = total + jnp.concatenate([low, high], axis=0)
    return part[...] - scale[:, 1:2] * total, fetched


def combine_kernel(*refs):
    outside, inverse, outs, inside = refs[:7], refs[7], refs[8:13], refs[13:19]
    arrived, inv, blocks, w, u, planes, rows, sent = refs[19:]
    image, fetched = image_of(outside, inside, arrived, (inverse, inv, blocks))
    precondition(inside[0], fetched, inv, image, inside[5], *outs, w, u, planes, rows, sent)


def last_kernel(*refs):
    outside, basis, lines, out, inside = refs[:7], refs[7:11], refs[11:15], refs[15], refs[16:22]
    arrived, held, sums, landed = refs[22:]
    pairs = [(basis[k], held.at[k]) for k in range(ITERS)]
    pairs += [(lines[k], sums.at[k]) for k in range(ITERS)]
    copies = start(pairs, landed)
    image, _ = image_of(outside, inside, arrived)
    for copy in copies:
        copy.wait()
    line = dots([held[k] for k in range(ITERS)], image)
    for k in range(ITERS):
        line = line + sums[k]
    out[...] = jnp.broadcast_to(line[0:1], out.shape)


def solve(gram, shift):
    def g(a, b):
        return gram[(max(a, b), min(a, b))]

    n = ITERS
    target = [g(a + 1, 0) + shift * g(a, 0) for a in range(n)]
    normal = {}
    for a in range(n):
        for b in range(a + 1):
            normal[a, b] = (
                g(a + 1, b + 1) + shift * (g(a + 1, b) + g(a, b + 1)) + shift * shift * g(a, b)
            )
    size = [lax.rsqrt(normal[a, a]) for a in range(n)]
    target = [target[a] * size[a] for a in range(n)]
    lower = {}
    inverse = [None] * n
    for a in range(n):
        for b in range(a + 1):
            value = normal[a, b] * size[a] * size[b]
            for c in range(b):
                value = value - lower[a, c] * lower[b, c]
            if a == b:
                inverse[a] = lax.rsqrt(value)
            else:
                lower[a, b] = value * inverse[b]
    half = []
    for a in range(n):
        value = target[a]
        for c in range(a):
            value = value - lower[a, c] * half[c]
        half.append(value * inverse[a])
    result = [None] * n
    for a in reversed(range(n)):
        value = half[a]
        for c in range(a + 1, n):
            value = value - lower[c, a] * result[c]
        result[a] = value * inverse[a]
    return [result[a] * size[a] for a in range(n)]


def finish_kernel(*refs):
    n = ITERS
    outside, outs, inside = refs[: n + 4], refs[n + 4 : n + 6], refs[n + 6 : n + 11]
    arrived, result, mean, sent = refs[n + 11 :]
    lines, scale, meta, average, fields = inside
    copies = start(
        zip(outside, [lines, scale, meta, average] + [fields.at[k] for k in range(n)]), arrived
    )
    copies[0].wait()
    line = jnp.sum(lines[...], axis=0, keepdims=True)
    gram = {}
    k = 0
    for a in range(ITERS + 1):
        for b in range(a + 1):
            gram[a, b] = line[:, k : k + 1]
            k += 1
    copies[1].wait()
    weights = solve(gram, scale[0:1, 2:3])
    factor = scale[0:1, 4:5]
    for copy in copies[2:]:
        copy.wait()
    total = (weights[0] * factor) * fields[0]
    for k in range(1, ITERS):
        total = total + (weights[k] * factor) * fields[k]
    summed = total[:PAD] + total[PAD:]
    blank = jnp.zeros((64 - PAD, FACE), jnp.float32)
    spread = jnp.concatenate([summed, blank, summed, blank], axis=0)
    weight = average[...].astype(jnp.bfloat16)
    got = lax.dot_general(
        jnp.concatenate([weight, weight], axis=1),
        jnp.concatenate(two(spread), axis=1),
        NT,
        preferred_element_type=jnp.float32,
    )
    lane = lax.broadcasted_iota(jnp.int32, (32, 128), 1)
    mean[...] = jnp.where(lane < 64, got[:32], got[32:])
    home = meta[4, meta[5, 0]] // 4
    copies = start([(mean, outs[1].at[home])], sent)
    species = result.shape[0]
    result[:, 0, :] = total[:species]
    result[:, 1, :] = total[PAD : PAD + species]
    copies.append(pltpu.make_async_copy(result, outs[0], sent.at[1]))
    copies[1].start()
    for copy in copies:
        copy.wait()


def update_kernel(*refs):
    outside, out, inside, arrived = refs[:4], refs[4], refs[5:9], refs[9]
    copies = start(zip(outside, inside), arrived)
    for copy in copies:
        copy.wait()
    sources, received, patch, halves = inside
    lane = lax.broadcasted_iota(jnp.int32, (1, FACE), 1)
    covered = jnp.zeros((1, FACE), jnp.int32)
    blocks = []
    for m in range(4):
        source = sources[0, m]
        block = received[jnp.maximum(source, 0)]
        blocks.append(jnp.where(jnp.full((32, 128), source, jnp.int32) >= 0, block, 0.0))
        covered = jnp.where(lane // 64 == m, source, covered)
    stacked = jnp.concatenate(blocks, axis=0)
    species = patch.shape[0]
    half = halves[...].astype(jnp.bfloat16)
    got = lax.dot_general(
        jnp.concatenate(two(stacked), axis=0),
        jnp.concatenate([half, half], axis=0),
        TN,
        preferred_element_type=jnp.float32,
    )
    got = got[0:species, :FACE] + got[64 : 64 + species, FACE:]
    out[:, 0, :] = jnp.where(covered >= 0, got, patch[:, 0, :])


def on_device(
    source_term,
    diffusion,
    stoich,
    orders,
    rates,
    precond,
    coarse_field,
    neighbours,
    ghost_list,
    average_list,
):
    species, reactions = stoich.shape
    groups = lax.axis_size("grp")
    boxes = lax.axis_size("box")
    me = lax.axis_index("grp")
    box = lax.axis_index("box")
    f32 = jnp.float32

    ids = jnp.stack([me, box, jnp.asarray(boxes - 1, box.dtype)]).astype(jnp.int32)
    links = neighbours.T
    owned = average_list.T
    even_swap = [(i, i ^ 1) for i in range(boxes)]
    odd_swap = [(i, (i + (1 if i % 2 else -1)) % boxes) for i in range(boxes)]

    meta = jnp.concatenate([links, owned, jnp.pad(ids, (0, groups - 3))[None]], axis=0)
    meta = jnp.pad(meta, ((0, 2), (0, 128 - groups)))

    def exchange(slots):
        return lax.all_to_all(slots, "grp", 0, 0, tiled=True)

    (asked,) = call(
        gather_kernel,
        "gather",
        [(groups, SLOT, 128)],
        (ids, coarse_field, ghost_list),
        [SMEM] + [HBM] * 2,
        [
            pltpu.VMEM(coarse_field.shape, f32),
            pltpu.VMEM(ghost_list.shape, jnp.int32),
            pltpu.SemaphoreType.DMA((2,)),
            pltpu.VMEM((groups * SLOT, 2 * FACE), jnp.bfloat16),
            pltpu.VMEM((groups, SLOT, 128), f32),
            pltpu.SemaphoreType.DMA((groups // 8,)),
        ],
        [HBM],
        WHOLE,
    )
    received = exchange(asked)
    scale, stoich_s, orders_s, sources = call(
        prepare_kernel,
        "prepare",
        [(ROWS, 128), (2 * PAD, reactions, jnp.bfloat16), (reactions, 3 * PAD, jnp.bfloat16), (8, 128, jnp.int32)],
        (ids, owned, diffusion.reshape(1, species), stoich, orders.T),
        [SMEM] + [VMEM] * 4,
        (),
        [VMEM] * 3 + [SMEM],
        WHOLE,
    )
    rates_s = jnp.moveaxis(rates[:, 0], 1, 0)
    inverse = precond.reshape(species, 2 * species, FACE)
    source, rates_s = lax.optimization_barrier((source_term.reshape(2 * species, FACE), rates_s))
    faces = jnp.asarray(FACES)
    inside = jnp.asarray(INSIDE)
    outs = [(ROWS, FACE), (PAD, FACE), (PAD, FACE), (ROWS, FACE), (groups, FS, 128)]
    cells = pltpu.VMEM((ROWS, FACE), f32)
    rows = [pltpu.VMEM((2, ROWS, 128), f32)]
    held = [pltpu.VMEM(inverse.shape, inverse.dtype), pltpu.SemaphoreType.DMA((PAD // 8,))]
    work = [cells, cells, pltpu.VMEM((4 * FS, 128), f32)] + rows + [pltpu.SemaphoreType.DMA((8,))]
    landing = [
        pltpu.SMEM(meta.shape, jnp.int32),
        pltpu.VMEM((groups, FS, 128), f32),
        pltpu.VMEM((2, PAD, FACE), f32),
        cells,
        pltpu.VMEM((ROWS, 128), f32),
        pltpu.VMEM((4 * FS, FACE), f32),
        pltpu.SemaphoreType.DMA((7,)),
    ]
    w, near, far, u, slots = call(
        first_kernel,
        "first",
        outs,
        (meta, received, source, scale, faces, inverse),
        [HBM] * 6,
        [pltpu.SMEM(meta.shape, jnp.int32)]
        + [pltpu.VMEM(x.shape, f32) for x in (received, source, scale, faces)]
        + [pltpu.SemaphoreType.DMA((5,))]
        + held
        + work,
        [HBM] * 5,
        WHOLE,
    )
    basis, directions, lines = [w], [u], []
    for j in range(ITERS):
        received = exchange(slots)
        near_in = lax.ppermute(near, "box", even_swap)
        far_in = lax.ppermute(far, "box", odd_swap)
        operands = (u, w, scale, inside, orders_s, stoich_s, rates_s) + tuple(basis[:-1])
        count = len(operands)
        part, line = call(
            functools.partial(local_kernel, j),
            "local%d" % j,
            [(ROWS, FACE), (8, 128)],
            operands,
            [HBM] * count,
            [pltpu.VMEM(x.shape, x.dtype) for x in operands]
            + [cells, pltpu.VMEM((8, 128), f32)]
            + [pltpu.SemaphoreType.DMA((count,)), pltpu.SemaphoreType.DMA((2,))],
            [HBM] * 2,
            WHOLE,
        )
        lines.append(line)
        shared = (meta, received, near_in, far_in, part, scale, faces)
        if j + 1 < ITERS:
            w, near, far, u, slots = call(
                combine_kernel,
                "combine%d" % j,
                outs,
                shared + (inverse,),
                [HBM] * 8,
                landing + held + work,
                [HBM] * 5,
                WHOLE,
            )
            basis.append(w)
            directions.append(u)
        else:
            (lines,) = call(
                last_kernel,
                "last",
                [(groups * boxes, 128)],
                shared + tuple(basis) + tuple(lines),
                [HBM] * 15,
                landing
                + [pltpu.VMEM((ITERS, ROWS, FACE), f32), pltpu.VMEM((ITERS, 8, 128), f32)]
                + [pltpu.SemaphoreType.DMA((2 * ITERS,))],
                limit=WHOLE,
            )
    lines = lax.all_to_all(lines, ("grp", "box"), 0, 0, tiled=True)
    average = jnp.asarray(AVERAGE)
    correction, slots = call(
        finish_kernel,
        "finish",
        [(species, 2, FACE), (groups, 32, 128)],
        (lines, scale, meta, average) + tuple(directions),
        [HBM] * (4 + ITERS),
        [pltpu.VMEM(lines.shape, f32), pltpu.VMEM((ROWS, 128), f32)]
        + [pltpu.SMEM(meta.shape, jnp.int32), pltpu.VMEM(average.shape, f32)]
        + [pltpu.VMEM((ITERS, ROWS, FACE), f32), pltpu.SemaphoreType.DMA((ITERS + 4,))]
        + [pltpu.VMEM((species, 2, FACE), f32), pltpu.VMEM((32, 128), f32)]
        + [pltpu.SemaphoreType.DMA((2,))],
        [HBM] * 2,
        WHOLE,
    )
    received = exchange(slots)
    received, correction = lax.optimization_barrier((received, correction))
    halves = jnp.asarray(HALVES)
    (updated,) = call(
        update_kernel,
        "update",
        [(species, 1, FACE)],
        (sources, received, coarse_field, halves),
        [HBM] * 4,
        [pltpu.SMEM((8, 128), jnp.int32), pltpu.VMEM(received.shape, f32)]
        + [pltpu.VMEM(coarse_field.shape, f32), pltpu.VMEM(halves.shape, f32)]
        + [pltpu.SemaphoreType.DMA((4,))],
        limit=WHOLE,
    )
    return correction.reshape(species, 1, 2, FACE), updated


def solution(mesh):
    placed = (
        P(None, "grp", "box", None),
        P(),
        P(),
        P(),
        P(None, "grp", "box", None),
        P(None, None, "grp", "box", None),
        P(None, "grp", "box"),
        P(),
        P(None, "box", None),
        P(None, "box"),
    )
    return jax.shard_map(
        on_device,
        mesh=mesh,
        in_specs=placed,
        out_specs=(P(None, "grp", "box", None), P(None, "grp", "box")),
        check_vma=False,
    )
```

```python
import functools

import jax
import jax.numpy as jnp
import numpy as np
from jax import lax
from jax.experimental import pallas as pl
from jax.experimental.pallas import tpu as pltpu
from jax.sharding import PartitionSpec as P

FS = 16
ITERS = 4
SHIFT = 1.0
HALF = FS // 2
FACE = FS * FS
PAD = 56
ROWS = 2 * PAD
SLOT = 40
WHOLE = 66900000
EXACT = lax.Precision.HIGHEST
HBM = pl.BlockSpec(memory_space=pltpu.HBM)
VMEM = pl.BlockSpec(memory_space=pltpu.VMEM)
SMEM = pl.BlockSpec(memory_space=pltpu.SMEM)

NN = (((1,), (0,)), ((), ()))
NT = (((1,), (1,)), ((), ()))
TN = (((0,), (0,)), ((), ()))


def mm(a, b, dims=NN):
    return lax.dot_general(a, b, dims, precision=EXACT, preferred_element_type=jnp.float32)


def two(value):
    high = value.astype(jnp.bfloat16)
    return high, (value - high.astype(jnp.float32)).astype(jnp.bfloat16)


def select(a, b):
    parts = jnp.concatenate(two(a), axis=0)
    got = lax.dot_general(parts, b, NN, preferred_element_type=jnp.float32)
    return got[: a.shape[0]] + got[a.shape[0] :]


def constants():
    cell = np.arange(FACE)
    y, z = cell // FS, cell % FS
    t = np.arange(FS)
    faces = np.zeros((4 * FS, FACE), np.float32)
    for f, lanes in enumerate((t, FACE - FS + t, t * FS, t * FS + FS - 1)):
        faces[f * FS + t, lanes] = 1.0
    inside = np.zeros((FACE, FACE), np.float32)
    for dy, dz in ((1, 0), (-1, 0), (0, 1), (0, -1)):
        ok = (y + dy >= 0) & (y + dy < FS) & (z + dz >= 0) & (z + dz < FS)
        inside[cell[ok], (y + dy)[ok] * FS + (z + dz)[ok]] = 1.0
    coarse = y // 2 * HALF + z // 2
    upsample = np.zeros((HALF * HALF, FACE), np.float32)
    upsample[coarse, cell] = 1.0
    halves = np.zeros((128, 2 * FACE), np.float32)
    for m in range(4):
        c = np.arange(32)
        halves[32 * m + c, 64 * m + c] = 1.0
        halves[32 * m + c, FACE + 64 * m + 32 + c] = 1.0
    return faces, inside, upsample * 0.125, halves


FACES, INSIDE, AVERAGE, HALVES = constants()


def call(kernel, name, shapes, args, specs, scratch=(), out_specs=None, limit=24 << 20):
    return pl.pallas_call(
        kernel,
        out_shape=[
            jax.ShapeDtypeStruct(s[:-1], s[-1])
            if not isinstance(s[-1], int)
            else jax.ShapeDtypeStruct(s, jnp.float32)
            for s in shapes
        ],
        in_specs=specs,
        out_specs=out_specs or [VMEM] * len(shapes),
        scratch_shapes=list(scratch),
        compiler_params=pltpu.CompilerParams(vmem_limit_bytes=limit),
        name=name,
    )(*args)


def split(value):
    high = value.astype(jnp.bfloat16)
    rest = value - high.astype(jnp.float32)
    middle = rest.astype(jnp.bfloat16)
    low = (rest - middle.astype(jnp.float32)).astype(jnp.bfloat16)
    return high, middle, low


def gather_kernel(ids, patch_out, lists_out, out, patch, lists, arrived, hot, slots, sent):
    copies = start([(patch_out, patch), (lists_out, lists)], arrived)
    for copy in copies:
        copy.wait()
    species = patch.shape[0]
    row = lax.broadcasted_iota(jnp.int32, (species, FACE), 0)
    lane = lax.broadcasted_iota(jnp.int32, (species, FACE), 1)
    place = ((lane == row) | (lane == row + 192)).astype(jnp.float32)
    turned = mm(patch[:, 0, :], place, TN)
    parts = jnp.concatenate(
        [jnp.concatenate(split(turned[:, 128 * h : 128 * h + 128]), axis=1) for h in range(2)],
        axis=0,
    )
    entries = lists[:, 0, :].astype(jnp.float32) - (ids[0] * FACE).astype(jnp.float32)
    across = entries[:, 0:128].T
    beside = entries[:, 128:160].T
    entries = jnp.concatenate(
        [
            jnp.maximum(across[0:64], across[64:128]),
            jnp.maximum(beside[0:8], beside[8:16]),
            jnp.maximum(beside[16:24], beside[24:32]),
        ],
        axis=0,
    )
    cell = lax.broadcasted_iota(jnp.int32, (SLOT, FACE), 1).astype(jnp.float32)
    groups = out.shape[0]
    for g in range(0, groups, 2):
        pair = [
            jnp.concatenate(
                [
                    (cell == entries[SLOT * h : SLOT * h + SLOT, k : k + 1]).astype(jnp.float32)
                    for h in range(2)
                ],
                axis=1,
            )
            for k in (g, g + 1)
        ]
        hot[SLOT * g : SLOT * g + 2 * SLOT, :] = jnp.concatenate(pair, axis=0).astype(jnp.bfloat16)
    step = 8
    copies = []
    for g in range(0, groups, step):
        got = jnp.dot(
            hot[SLOT * g : SLOT * (g + step), :], parts, preferred_element_type=jnp.float32
        )
        got = got[:, 0:128] + got[:, 128:256] + got[:, 256:384]
        for k in range(step):
            slots[g + k] = got[SLOT * k : SLOT * k + SLOT]
        part = pl.ds(g, step)
        copies.append(pltpu.make_async_copy(slots.at[part], out.at[part], sent.at[g // step]))
        copies[-1].start()
    for copy in copies:
        copy.wait()


def prepare_kernel(ids, owned, diffusion, stoich, orders, scale, stoich_out, orders_out, sources):
    me = ids[0]
    group = lax.broadcasted_iota(jnp.int32, owned.shape, 1)
    for m in range(4):
        sources[0, m] = jnp.max(jnp.where(owned[...] == me * 4 + m, group, -1))
    d = diffusion[...]
    species = d.shape[1]
    row = lax.broadcasted_iota(jnp.int32, (PAD, species), 0)
    lane = lax.broadcasted_iota(jnp.int32, (PAD, species), 1)
    column = jnp.sum(jnp.where(row == lane, d, 0.0), axis=1, keepdims=True)

    def total(value):
        return jnp.sum(jnp.sum(value, axis=0, keepdims=True), axis=1, keepdims=True)

    wide = 1.0 + 12.0 * jnp.max(column, axis=0, keepdims=True)
    s, o = stoich[...], orders[...]
    wide = wide + jnp.sqrt(total(s * s)) * jnp.sqrt(total(o * o))
    unit = 32.0 / wide
    reactions = s.shape[1]
    high, low = two(jnp.concatenate([s * unit, jnp.zeros((PAD - species, reactions))], axis=0))
    stoich_out[...] = jnp.concatenate([high, low], axis=0)
    o = jnp.concatenate([o, jnp.zeros((PAD - species, reactions))], axis=0).T
    high, low = two(o)
    orders_out[...] = jnp.concatenate([high, high, low], axis=1)
    lane = lax.broadcasted_iota(jnp.int32, (PAD, 128), 1)
    row = lax.broadcasted_iota(jnp.int32, (PAD, 1), 0)
    diagonal = jnp.where(row < species, unit * (1.0 + 6.0 * column), 0.0)
    value = jnp.where(lane == 0, diagonal, 0.0)
    value = jnp.where(lane == 1, unit * column, value)
    value = jnp.where(lane == 2, SHIFT * unit, value)
    value = jnp.where(lane == 3, column, value)
    value = jnp.where(lane == 4, unit, value)
    scale[0:PAD, :] = value
    scale[PAD:, :] = value


def mix(a, b, keep, shift):
    return jnp.where(keep, a, b) + pltpu.roll(jnp.where(keep, b, a), shift, 0)


def fetch(inverse, inv, arrived):
    count = inverse.shape[0]
    copies = []
    for block in range(PAD // 8):
        part = pl.ds(8 * block, min(8, count - 8 * block))
        copies.append(pltpu.make_async_copy(inverse.at[part], inv.at[part], arrived.at[block]))
    for copy in copies:
        copy.start()
    return copies


def apply_inverse(copies, inv, rows, u):
    count, depth = inv.shape[0], inv.shape[1]
    full = depth // 8
    row = lax.broadcasted_iota(jnp.int32, (8, 128), 0)
    bit2, bit1, bit0 = (row & 4) == 0, (row & 2) == 0, (row & 1) == 0
    zero = jnp.zeros((8, 128), jnp.float32)
    for block in range(PAD // 8):
        copies[block].wait()
        for half in range(2):
            lanes = slice(128 * half, 128 * half + 128)
            w = [rows[half, 8 * k : 8 * k + 8, :] for k in range(full + 1)]

            def one(i):
                if i >= count:
                    return zero
                m = inv[i, :, lanes].astype(jnp.float32)
                total = m[0:8] * w[0]
                for k in range(1, full):
                    total = total + m[8 * k : 8 * k + 8] * w[k]
                last = m[8 * full : depth]
                last = jnp.concatenate([last, zero[last.shape[0] :]], axis=0)
                return total + last * w[full]

            a = [one(8 * block + d) for d in range(8)]
            b = [mix(a[d], a[d + 2], bit1, 6) for d in (0, 1, 4, 5)]
            c = [mix(b[d], b[d + 2], bit2, 4) for d in range(2)]
            u[8 * block : 8 * block + 8, lanes] = jnp.where(bit0, c[0], pltpu.roll(c[1], 1, 0))
            u[PAD + 8 * block : PAD + 8 * block + 8, lanes] = jnp.where(
                bit0, pltpu.roll(c[0], 7, 0), c[1]
            )


def interleave(rows, field):
    for half in range(2):
        lanes = slice(128 * half, 128 * half + 128)
        rows.at[half][pl.ds(0, PAD, stride=2), :] = field[:PAD, lanes]
        rows.at[half][pl.ds(1, PAD, stride=2), :] = field[PAD:, lanes]


def separate(rows):
    planes = [
        jnp.concatenate([rows.at[h][pl.ds(x, PAD, stride=2), :] for h in range(2)], axis=1)
        for x in range(2)
    ]
    return jnp.concatenate(planes, axis=0)


def start(pairs, semaphores):
    copies = [
        pltpu.make_async_copy(source, target, semaphores.at[k])
        for k, (source, target) in enumerate(pairs)
    ]
    for copy in copies:
        copy.start()
    return copies


def precondition(meta, fetched, inv, image, faces, w_out, near, far, u_out, slots, w, u, planes, rows, sent):
    w[...] = image
    copies = [pltpu.make_async_copy(w, w_out, sent.at[0])]
    copies[0].start()
    interleave(rows, image)
    apply_inverse(fetched, inv, rows, u)
    even = meta[5, 1] % 2
    lower = pl.multiple_of(even * PAD, 8)
    upper = pl.multiple_of(PAD - even * PAD, 8)
    copies.append(pltpu.make_async_copy(u.at[pl.ds(upper, PAD)], near, sent.at[1]))
    copies.append(pltpu.make_async_copy(u.at[pl.ds(lower, PAD)], far, sent.at[2]))
    copies.append(pltpu.make_async_copy(u, u_out, sent.at[3]))
    for copy in copies[1:]:
        copy.start()
    face = faces[...].astype(jnp.bfloat16)
    planes[:, 0:ROWS] = lax.dot_general(
        jnp.concatenate([face, face], axis=1),
        jnp.concatenate(two(u[...]), axis=1),
        NT,
        preferred_element_type=jnp.float32,
    )
    for f in range(4):
        other = meta[f, meta[5, 0]]

        @pl.when(other >= 0)
        def _():
            pltpu.make_async_copy(
                planes.at[pl.ds(FS * f, FS)], slots.at[jnp.maximum(other, 0)], sent.at[4 + f]
            ).start()

    for f in range(4):
        other = meta[f, meta[5, 0]]

        @pl.when(other >= 0)
        def _():
            pltpu.make_async_copy(
                planes.at[pl.ds(FS * f, FS)], slots.at[jnp.maximum(other, 0)], sent.at[4 + f]
            ).wait()

    for copy in copies:
        copy.wait()


def first_kernel(*refs):
    outside, inverse, outs, inside = refs[:5], refs[5], refs[6:11], refs[11:16]
    arrived, inv, blocks, w, u, planes, rows, sent = refs[16:]
    copies = start(zip(outside, inside), arrived)
    fetched = fetch(inverse, inv, blocks)
    for copy in copies:
        copy.wait()
    meta, received, source, scale, faces = inside
    values = received[0]
    for g in range(1, received.shape[0]):
        values = values + received[g]
    me = meta[5, 0]
    row = lax.broadcasted_iota(jnp.int32, (SLOT, FACE), 0)
    cell = lax.broadcasted_iota(jnp.int32, (SLOT, FACE), 1)
    y, z = cell // FS, cell % FS
    coarse = y // 2 * HALF + z // 2
    first = 64 - SLOT
    y_face = jnp.where(meta[0, me] < 0, 0, FS - 1)
    z_face = jnp.where(meta[2, me] < 0, 0, FS - 1)
    sides = ((y == y_face) & (row == first + z // 2)).astype(jnp.float32)
    sides = sides + ((z == z_face) & (row == first + HALF + y // 2)).astype(jnp.float32)
    ends = [coarse == row, (coarse == row + SLOT) & (row < first)]
    ends = [end.astype(jnp.float32) for end in ends]
    across = mm(values, jnp.concatenate([ends[0], ends[1], sides], axis=1), TN)
    beside = across[64 : 64 + PAD, 2 * FACE :]
    across = across[0:PAD, :FACE] + across[64 : 64 + PAD, FACE : 2 * FACE]
    bottom = jnp.where(meta[5, 1] == 0, 1.0, 0.0)
    boundary = jnp.concatenate([beside + bottom * across, beside + (1.0 - bottom) * across], axis=0)
    species = source.shape[0]
    for half in range(2):
        rows[half, 0:species, :] = source[:, 128 * half : 128 * half + 128]
        rows[half, species:ROWS, :] = jnp.zeros((ROWS - species, 128), jnp.float32)
    right = separate(rows) + scale[:, 3:4] * boundary
    precondition(meta, fetched, inv, right, faces, *outs, w, u, planes, rows, sent)


def dots(vectors, last):
    lane = lax.broadcasted_iota(jnp.int32, (8, 128), 1)
    line = jnp.zeros((8, 128), jnp.float32)
    count = len(vectors)
    for b, vector in enumerate(vectors + [last]):
        product = last * vector
        total = product[0:8]
        for k in range(8, ROWS, 8):
            total = total + product[k : k + 8]
        total = jnp.sum(total[:, :128] + total[:, 128:], axis=0, keepdims=True)
        total = jnp.sum(total, axis=1, keepdims=True)
        line = jnp.where(lane == count * (count + 1) // 2 + b, total, line)
    return line


def local_kernel(j, *refs):
    count = 7 + j
    outside, (part, line), inside_refs = refs[:count], refs[count : count + 2], refs[count + 2 :]
    result, summed, arrived, sent = inside_refs[count:]
    copies = start(zip(outside, inside_refs[:count]), arrived)
    u, w, scale, inside, orders, stoich, rates = inside_refs[:7]
    for copy in copies:
        copy.wait()
    field = u[...]
    lower, upper = field[:PAD], field[PAD:]
    total = select(field, inside[...].astype(jnp.bfloat16))
    total = total + jnp.concatenate([field[PAD:], field[:PAD]], axis=0)
    both = jnp.concatenate([lower, upper], axis=1)
    high, low = two(both)
    progress = jnp.dot(
        orders[...], jnp.concatenate([high, low, high], axis=0), preferred_element_type=jnp.float32
    )
    progress = [progress[:, FACE * x : FACE * x + FACE] * rates[x] for x in range(2)]
    high, low = two(jnp.concatenate(progress, axis=1))
    chemistry = jnp.dot(stoich[...], high, preferred_element_type=jnp.float32)
    chemistry = chemistry[:PAD] + chemistry[PAD:]
    rest = jnp.dot(stoich[...], low, preferred_element_type=jnp.float32)
    chemistry = chemistry + rest[:PAD]
    chemistry = jnp.concatenate([chemistry[:, :FACE], chemistry[:, FACE:]], axis=0)
    result[...] = (
        scale[:, 0:1] * field - scale[:, 1:2] * total - chemistry - scale[:, 2:3] * w[...]
    )
    copies = start([(result, part)], sent)
    summed[...] = dots([ref[...] for ref in inside_refs[7:count]], w[...])
    copy = pltpu.make_async_copy(summed, line, sent.at[1])
    copy.start()
    copy.wait()
    copies[0].wait()


def image_of(outside, inside, arrived, blocks=None):
    meta, received, ends, part, scale, faces = inside
    targets = (meta, received, ends.at[0], ends.at[1], part, scale, faces)
    copies = start(zip(outside, targets), arrived)
    fetched = fetch(*blocks) if blocks else None
    for copy in copies:
        copy.wait()
    me, box = meta[5, 0], meta[5, 1]
    ghosts = []
    for f in range(4):
        other = meta[f, me]
        plane = received[jnp.maximum(other, 0), :, 0:ROWS]
        ghosts.append(jnp.where(jnp.full((FS, ROWS), other, jnp.int32) >= 0, plane, 0.0))
    face = faces[...].astype(jnp.bfloat16)
    total = lax.dot_general(
        jnp.concatenate(two(jnp.concatenate(ghosts, axis=0)), axis=0),
        jnp.concatenate([face, face], axis=0),
        TN,
        preferred_element_type=jnp.float32,
    )
    even = 1 - box % 2
    low = jnp.where(box == 0, 0.0, 1.0) * ends[even]
    high = jnp.where(box == meta[5, 2], 0.0, 1.0) * ends[1 - even]
    total = total + jnp.concatenate([low, high], axis=0)
    return part[...] - scale[:, 1:2] * total, fetched


def combine_kernel(*refs):
    outside, inverse, outs, inside = refs[:7], refs[7], refs[8:13], refs[13:19]
    arrived, inv, blocks, w, u, planes, rows, sent = refs[19:]
    image, fetched = image_of(outside, inside, arrived, (inverse, inv, blocks))
    precondition(inside[0], fetched, inv, image, inside[5], *outs, w, u, planes, rows, sent)


def last_kernel(*refs):
    outside, basis, lines, out, inside = refs[:7], refs[7:11], refs[11:15], refs[15], refs[16:22]
    arrived, held, sums, landed = refs[22:]
    pairs = [(basis[k], held.at[k]) for k in range(ITERS)]
    pairs += [(lines[k], sums.at[k]) for k in range(ITERS)]
    copies = start(pairs, landed)
    image, _ = image_of(outside, inside, arrived)
    for copy in copies:
        copy.wait()
    line = dots([held[k] for k in range(ITERS)], image)
    for k in range(ITERS):
        line = line + sums[k]
    out[...] = jnp.broadcast_to(line[0:1], out.shape)


def solve(gram, shift):
    def g(a, b):
        return gram[(max(a, b), min(a, b))]

    n = ITERS
    target = [g(a + 1, 0) + shift * g(a, 0) for a in range(n)]
    normal = {}
    for a in range(n):
        for b in range(a + 1):
            normal[a, b] = (
                g(a + 1, b + 1) + shift * (g(a + 1, b) + g(a, b + 1)) + shift * shift * g(a, b)
            )
    size = [lax.rsqrt(normal[a, a]) for a in range(n)]
    target = [target[a] * size[a] for a in range(n)]
    lower = {}
    inverse = [None] * n
    for a in range(n):
        for b in range(a + 1):
            value = normal[a, b] * size[a] * size[b]
            for c in range(b):
                value = value - lower[a, c] * lower[b, c]
            if a == b:
                inverse[a] = lax.rsqrt(value)
            else:
                lower[a, b] = value * inverse[b]
    half = []
    for a in range(n):
        value = target[a]
        for c in range(a):
            value = value - lower[a, c] * half[c]
        half.append(value * inverse[a])
    result = [None] * n
    for a in reversed(range(n)):
        value = half[a]
        for c in range(a + 1, n):
            value = value - lower[c, a] * result[c]
        result[a] = value * inverse[a]
    return [result[a] * size[a] for a in range(n)]


def finish_kernel(*refs):
    n = ITERS
    outside, outs, inside = refs[: n + 4], refs[n + 4 : n + 6], refs[n + 6 : n + 11]
    arrived, result, mean, sent = refs[n + 11 :]
    lines, scale, meta, average, fields = inside
    copies = start(
        zip(outside, [lines, scale, meta, average] + [fields.at[k] for k in range(n)]), arrived
    )
    copies[0].wait()
    line = jnp.sum(lines[...], axis=0, keepdims=True)
    gram = {}
    k = 0
    for a in range(ITERS + 1):
        for b in range(a + 1):
            gram[a, b] = line[:, k : k + 1]
            k += 1
    copies[1].wait()
    weights = solve(gram, scale[0:1, 2:3])
    factor = scale[0:1, 4:5]
    for copy in copies[2:]:
        copy.wait()
    total = (weights[0] * factor) * fields[0]
    for k in range(1, ITERS):
        total = total + (weights[k] * factor) * fields[k]
    summed = total[:PAD] + total[PAD:]
    blank = jnp.zeros((64 - PAD, FACE), jnp.float32)
    spread = jnp.concatenate([summed, blank, summed, blank], axis=0)
    weight = average[...].astype(jnp.bfloat16)
    got = lax.dot_general(
        jnp.concatenate([weight, weight], axis=1),
        jnp.concatenate(two(spread), axis=1),
        NT,
        preferred_element_type=jnp.float32,
    )
    lane = lax.broadcasted_iota(jnp.int32, (32, 128), 1)
    mean[...] = jnp.where(lane < 64, got[:32], got[32:])
    home = meta[4, meta[5, 0]] // 4
    copies = start([(mean, outs[1].at[home])], sent)
    species = result.shape[0]
    result[:, 0, :] = total[:species]
    result[:, 1, :] = total[PAD : PAD + species]
    copies.append(pltpu.make_async_copy(result, outs[0], sent.at[1]))
    copies[1].start()
    for copy in copies:
        copy.wait()


def update_kernel(*refs):
    outside, out, inside, arrived = refs[:4], refs[4], refs[5:9], refs[9]
    copies = start(zip(outside, inside), arrived)
    for copy in copies:
        copy.wait()
    sources, received, patch, halves = inside
    lane = lax.broadcasted_iota(jnp.int32, (1, FACE), 1)
    covered = jnp.zeros((1, FACE), jnp.int32)
    blocks = []
    for m in range(4):
        source = sources[0, m]
        block = received[jnp.maximum(source, 0)]
        blocks.append(jnp.where(jnp.full((32, 128), source, jnp.int32) >= 0, block, 0.0))
        covered = jnp.where(lane // 64 == m, source, covered)
    stacked = jnp.concatenate(blocks, axis=0)
    species = patch.shape[0]
    half = halves[...].astype(jnp.bfloat16)
    got = lax.dot_general(
        jnp.concatenate(two(stacked), axis=0),
        jnp.concatenate([half, half], axis=0),
        TN,
        preferred_element_type=jnp.float32,
    )
    got = got[0:species, :FACE] + got[64 : 64 + species, FACE:]
    out[:, 0, :] = jnp.where(covered >= 0, got, patch[:, 0, :])


def on_device(
    source_term,
    diffusion,
    stoich,
    orders,
    rates,
    precond,
    coarse_field,
    neighbours,
    ghost_list,
    average_list,
):
    species, reactions = stoich.shape
    groups = lax.axis_size("grp")
    boxes = lax.axis_size("box")
    me = lax.axis_index("grp")
    box = lax.axis_index("box")
    f32 = jnp.float32

    ids = jnp.stack([me, box, jnp.asarray(boxes - 1, box.dtype)]).astype(jnp.int32)
    links = neighbours.T
    owned = average_list.T
    even_swap = [(i, i ^ 1) for i in range(boxes)]
    odd_swap = [(i, (i + (1 if i % 2 else -1)) % boxes) for i in range(boxes)]

    meta = jnp.concatenate([links, owned, jnp.pad(ids, (0, groups - 3))[None]], axis=0)
    meta = jnp.pad(meta, ((0, 2), (0, 128 - groups)))

    def exchange(slots):
        return lax.all_to_all(slots, "grp", 0, 0, tiled=True)

    (asked,) = call(
        gather_kernel,
        "gather",
        [(groups, SLOT, 128)],
        (ids, coarse_field, ghost_list),
        [SMEM] + [HBM] * 2,
        [
            pltpu.VMEM(coarse_field.shape, f32),
            pltpu.VMEM(ghost_list.shape, jnp.int32),
            pltpu.SemaphoreType.DMA((2,)),
            pltpu.VMEM((groups * SLOT, 2 * FACE), jnp.bfloat16),
            pltpu.VMEM((groups, SLOT, 128), f32),
            pltpu.SemaphoreType.DMA((groups // 8,)),
        ],
        [HBM],
        WHOLE,
    )
    received = exchange(asked)
    scale, stoich_s, orders_s, sources = call(
        prepare_kernel,
        "prepare",
        [(ROWS, 128), (2 * PAD, reactions, jnp.bfloat16), (reactions, 3 * PAD, jnp.bfloat16), (8, 128, jnp.int32)],
        (ids, owned, diffusion.reshape(1, species), stoich, orders.T),
        [SMEM] + [VMEM] * 4,
        (),
        [VMEM] * 3 + [SMEM],
        WHOLE,
    )
    rates_s = jnp.moveaxis(rates[:, 0], 1, 0)
    inverse = precond.reshape(species, 2 * species, FACE)
    source, rates_s = lax.optimization_barrier((source_term.reshape(2 * species, FACE), rates_s))
    faces = jnp.asarray(FACES)
    inside = jnp.asarray(INSIDE)
    outs = [(ROWS, FACE), (PAD, FACE), (PAD, FACE), (ROWS, FACE), (groups, FS, 128)]
    cells = pltpu.VMEM((ROWS, FACE), f32)
    rows = [pltpu.VMEM((2, ROWS, 128), f32)]
    held = [pltpu.VMEM(inverse.shape, inverse.dtype), pltpu.SemaphoreType.DMA((PAD // 8,))]
    work = [cells, cells, pltpu.VMEM((4 * FS, 128), f32)] + rows + [pltpu.SemaphoreType.DMA((8,))]
    landing = [
        pltpu.SMEM(meta.shape, jnp.int32),
        pltpu.VMEM((groups, FS, 128), f32),
        pltpu.VMEM((2, PAD, FACE), f32),
        cells,
        pltpu.VMEM((ROWS, 128), f32),
        pltpu.VMEM((4 * FS, FACE), f32),
        pltpu.SemaphoreType.DMA((7,)),
    ]
    w, near, far, u, slots = call(
        first_kernel,
        "first",
        outs,
        (meta, received, source, scale, faces, inverse),
        [HBM] * 6,
        [pltpu.SMEM(meta.shape, jnp.int32)]
        + [pltpu.VMEM(x.shape, f32) for x in (received, source, scale, faces)]
        + [pltpu.SemaphoreType.DMA((5,))]
        + held
        + work,
        [HBM] * 5,
        WHOLE,
    )
    basis, directions, lines = [w], [u], []
    for j in range(ITERS):
        received = exchange(slots)
        near_in = lax.ppermute(near, "box", even_swap)
        far_in = lax.ppermute(far, "box", odd_swap)
        operands = (u, w, scale, inside, orders_s, stoich_s, rates_s) + tuple(basis[:-1])
        count = len(operands)
        part, line = call(
            functools.partial(local_kernel, j),
            "local%d" % j,
            [(ROWS, FACE), (8, 128)],
            operands,
            [HBM] * count,
            [pltpu.VMEM(x.shape, x.dtype) for x in operands]
            + [cells, pltpu.VMEM((8, 128), f32)]
            + [pltpu.SemaphoreType.DMA((count,)), pltpu.SemaphoreType.DMA((2,))],
            [HBM] * 2,
            WHOLE,
        )
        lines.append(line)
        shared = (meta, received, near_in, far_in, part, scale, faces)
        if j + 1 < ITERS:
            w, near, far, u, slots = call(
                combine_kernel,
                "combine%d" % j,
                outs,
                shared + (inverse,),
                [HBM] * 8,
                landing + held + work,
                [HBM] * 5,
                WHOLE,
            )
            basis.append(w)
            directions.append(u)
        else:
            (lines,) = call(
                last_kernel,
                "last",
                [(groups * boxes, 128)],
                shared + tuple(basis) + tuple(lines),
                [HBM] * 15,
                landing
                + [pltpu.VMEM((ITERS, ROWS, FACE), f32), pltpu.VMEM((ITERS, 8, 128), f32)]
                + [pltpu.SemaphoreType.DMA((2 * ITERS,))],
                limit=WHOLE,
            )
    lines = lax.all_to_all(lines, ("grp", "box"), 0, 0, tiled=True)
    average = jnp.asarray(AVERAGE)
    correction, slots = call(
        finish_kernel,
        "finish",
        [(species, 2, FACE), (groups, 32, 128)],
        (lines, scale, meta, average) + tuple(directions),
        [HBM] * (4 + ITERS),
        [pltpu.VMEM(lines.shape, f32), pltpu.VMEM((ROWS, 128), f32)]
        + [pltpu.SMEM(meta.shape, jnp.int32), pltpu.VMEM(average.shape, f32)]
        + [pltpu.VMEM((ITERS, ROWS, FACE), f32), pltpu.SemaphoreType.DMA((ITERS + 4,))]
        + [pltpu.VMEM((species, 2, FACE), f32), pltpu.VMEM((32, 128), f32)]
        + [pltpu.SemaphoreType.DMA((2,))],
        [HBM] * 2,
        WHOLE,
    )
    received = exchange(slots)
    received, correction = lax.optimization_barrier((received, correction))
    halves = jnp.asarray(HALVES)
    (updated,) = call(
        update_kernel,
        "update",
        [(species, 1, FACE)],
        (sources, received, coarse_field, halves),
        [HBM] * 4,
        [pltpu.SMEM((8, 128), jnp.int32), pltpu.VMEM(received.shape, f32)]
        + [pltpu.VMEM(coarse_field.shape, f32), pltpu.VMEM(halves.shape, f32)]
        + [pltpu.SemaphoreType.DMA((4,))],
        limit=WHOLE,
    )
    return correction.reshape(species, 1, 2, FACE), updated


def solution(mesh):
    placed = (
        P(None, "grp", "box", None),
        P(),
        P(),
        P(),
        P(None, "grp", "box", None),
        P(None, None, "grp", "box", None),
        P(None, "grp", "box"),
        P(),
        P(None, "box", None),
        P(None, "box"),
    )
    return jax.shard_map(
        on_device,
        mesh=mesh,
        in_specs=placed,
        out_specs=(P(None, "grp", "box", None), P(None, "grp", "box")),
        check_vma=False,
    )
```
